32 devices in a mesh: dp: 8 (over z, y), mp: 4 (over x, core).
Axes of the slice: x: 2, y: 2, z: 4, core: 2. Of those that a mesh axis runs over, the one named last changes fastest.
Arguments:
- queries: bfloat16 [1024, 2048], P('dp', 'mp'), may hold values from -400 to 400
- encodings: bfloat16 [1024, 896], P('dp'), may hold values from -6 to 6
- kv_weight: bfloat16 [896, 2, 2048], P('dp', None, 'mp'), may hold values from -0.1875 to 0.1875
- pair_list: int32 [16, 2], P('dp'), may hold values from 0 to 7, as said below
- cotangent: bfloat16 [1024, 2048], P('dp', 'mp'), may hold values from -6 to 6
Outputs:
- attended: bfloat16 [1024, 2048], P('dp', 'mp')
- query_grad: bfloat16 [1024, 2048], P('dp', 'mp')
- encoding_grad: bfloat16 [1024, 896], P('dp', 'mp')
- weight_grad: float32 [896, 2, 2048], P('dp', None, 'mp')
The draws below stay inside these ranges and needn't reach their ends.
Inputs may be any that keep to these rules, and one draw needn't show every extreme that they name: Each dp device owns one neighbour block, block n belongs to dp device n, and pair_list[c, j] is at most 2 positions away from c // 2 along dp, counted around the cycle of 8 devices.
All inputs are finite; a program needn't handle non-finite values.
Results may differ from the reference program's by a relative error of at most 0.034.
The reference program's roundings to bfloat16 on the way count: a program that leaves them out, or rounds other values in their place, can miss the bound.
Values may be sent and summed in bfloat16 or wider, within the bound.
A program may use at most 64 MiB of HBM per device.

```python
import jax
import jax.numpy as jnp
from jax import lax

HEADS = 16
HD = 128
ENC = 896
SPAN = 64
NROWS = 128
NBR = 2
REACH = 2
CH_DEV = 2
SLOTS = 1
SPANS = 16
TOKENS = 1024
NEIGH = 8
N_DP = 8
N_MP = 4


def draw_queries(key, part):
    key = jax.random.fold_in(key, 11)
    first, second = jax.random.split(key)
    base = jax.random.normal(first, (TOKENS, HEADS * HD), jnp.float32)
    scales = jnp.exp(jax.random.uniform(second, (TOKENS, 1), jnp.float32, -0.5, 0.5))
    return jnp.clip(base * scales, -400.0, 400.0).astype(jnp.bfloat16)


def draw_pair_list(key, part):
    key = jax.random.fold_in(key, 23)
    first, second = jax.random.split(key)
    span_device = jnp.arange(SPANS, dtype=jnp.int32)[:, None] // CH_DEV
    offsets = jax.random.randint(first, (SPANS, NBR), -REACH, REACH + 1, dtype=jnp.int32)
    slot_draws = jax.random.randint(second, (SPANS, NBR, 2), 0, SLOTS, dtype=jnp.int32)
    slot_index = jnp.min(slot_draws, axis=-1)
    owners = (span_device + offsets) % N_DP
    block_ids = owners * SLOTS + slot_index
    block_ids = block_ids.at[0, 0].set(N_DP * SLOTS - 1).at[0, 1].set(0)
    return block_ids.astype(jnp.int32)


def spiked(entries, key, source, target, blocks, factor):
    def block_of(axis_at):
        return (jnp.arange(entries.shape[axis_at]) // (entries.shape[axis_at] // blocks)).reshape((-1,) + (1,) * (entries.ndim - 1 - axis_at))

    one_side = jax.random.permutation(key, blocks)[block_of(target)]
    second = (block_of(target) + blocks // 2) % blocks
    return jnp.where((block_of(source) == one_side) | (block_of(source) == second), factor * entries, entries)


def block_scale(key, dims, cuts, smallest, top_value):
    def one(position, blocks):
        heights = jax.random.uniform(jax.random.fold_in(jax.random.fold_in(key, 6), position), (blocks,), jnp.float32, smallest / len(cuts), top_value / len(cuts))
        return jnp.repeat(jnp.exp(heights), dims[position] // blocks).reshape((-1,) + (1,) * (len(dims) - position - 1))

    loudness = one(*cuts[0])
    for cut in cuts[1:]:
        loudness = loudness * one(*cut)
    return loudness


def normal_values(rng, shape, spread, limit, shards=(), kind=jnp.bfloat16):
    entries = spread * jax.random.normal(rng, shape, jnp.float32)
    if shards:
        entries = entries * block_scale(rng, shape, shards, -0.22, 0.18)
    return jnp.clip(entries, -limit, limit).astype(kind)


def noise_with(stream_key, shape, scale, limit, shards, heavy, kind=jnp.bfloat16):
    drawn = scale * jax.random.normal(stream_key, shape, jnp.float32)
    if shards:
        drawn = drawn * block_scale(stream_key, shape, shards, -0.22, 0.18)
    return jnp.clip(spiked(drawn, jax.random.fold_in(stream_key, 3), *heavy), -limit, limit).astype(kind)


def setup_inputs(seed: int = 0) -> dict:
    streams_of = jax.random.split(jax.random.key(seed), 6)
    queries = draw_queries(jax.random.fold_in(streams_of[5], 71), 0)
    encodings = noise_with(streams_of[1], (NEIGH * NROWS, ENC), 1.0, 6.0, ((0, 8),), (0, 1, 8, 2.0))
    kv_weight = normal_values(streams_of[2], (ENC, 2, HEADS * HD), ENC ** -0.5, 0.1875, ((0, 8), (2, 4)))
    pair_list = draw_pair_list(jax.random.fold_in(streams_of[5], 71), 0)
    cotangent = normal_values(streams_of[4], (TOKENS, HEADS * HD), 1.0, 6.0, ((0, 8), (1, 4)))
    return {"queries": queries, "encodings": encodings, "kv_weight": kv_weight, "pair_list": pair_list, "cotangent": cotangent}


def reference(queries, encodings, kv_weight, pair_list, cotangent):
    width = HEADS * HD
    factor = 1.0 / (HD ** 0.5)
    projected = jnp.einsum('re,etx->rtx', encodings.astype(jnp.float32), kv_weight.astype(jnp.float32), precision=lax.Precision.HIGHEST).astype(jnp.bfloat16)
    blocks = projected.reshape(NEIGH, NROWS, 2, HEADS, HD)
    query_groups = queries.reshape(N_DP, CH_DEV, SPAN, HEADS, HD)
    grad_groups = cotangent.reshape(N_DP, CH_DEV, SPAN, HEADS, HD)
    pair_groups = pair_list.reshape(N_DP, CH_DEV * NBR).astype(jnp.int32)

    def group(carry, inputs):
        query_rows, grad_rows, pair_ids = inputs
        chosen = blocks[pair_ids].reshape(CH_DEV, NBR * NROWS, 2, HEADS, HD)
        keys = chosen[:, :, 0].astype(jnp.float32)
        values = chosen[:, :, 1].astype(jnp.float32)
        query_f = query_rows.astype(jnp.float32)
        grad_f = grad_rows.astype(jnp.float32)
        scores = jnp.einsum('cqhd,ckhd->chqk', query_f, keys) * factor
        probs = jax.nn.softmax(scores, axis=-1)
        probs_b = probs.astype(jnp.bfloat16).astype(jnp.float32)
        attended = jnp.einsum('chqk,ckhd->cqhd', probs_b, values).astype(jnp.bfloat16)
        dprobs = jnp.einsum('cqhd,ckhd->chqk', grad_f, values)
        delta = jnp.sum(probs * dprobs, axis=-1, keepdims=True)
        dscores = (probs * (dprobs - delta) * factor).astype(jnp.bfloat16).astype(jnp.float32)
        query_grad = jnp.einsum('chqk,ckhd->cqhd', dscores, keys).astype(jnp.bfloat16)
        key_grad = jnp.einsum('chqk,cqhd->ckhd', dscores, query_f)
        value_grad = jnp.einsum('chqk,cqhd->ckhd', probs_b, grad_f)
        stacked = jnp.stack([key_grad, value_grad], axis=2).reshape(CH_DEV * NBR, NROWS, 2, HEADS, HD)
        carry = carry.at[pair_ids].add(stacked)
        return carry, (attended, query_grad)

    start = jnp.zeros((NEIGH, NROWS, 2, HEADS, HD), jnp.float32)
    block_grad, outputs = lax.scan(group, start, (query_groups, grad_groups, pair_groups))
    attended = outputs[0].reshape(TOKENS, width)
    query_grad = outputs[1].reshape(TOKENS, width)
    block_grad_b = block_grad.astype(jnp.bfloat16).reshape(NEIGH * NROWS, 2, width)
    grad_split = block_grad_b.astype(jnp.float32).reshape(NEIGH * NROWS, 2, N_MP, width // N_MP)
    weight_split = kv_weight.astype(jnp.float32).reshape(ENC, 2, N_MP, width // N_MP)
    partials = jnp.einsum('rtgx,etgx->gre', grad_split, weight_split, precision=lax.Precision.HIGHEST).astype(jnp.bfloat16)
    partials = lax.optimization_barrier(partials)
    encoding_grad = jnp.sum(partials.astype(jnp.float32), axis=0).astype(jnp.bfloat16)
    weight_grad = jnp.einsum('re,rtx->etx', encodings.astype(jnp.float32), block_grad_b.astype(jnp.float32), precision=lax.Precision.HIGHEST)
    return (attended, query_grad, encoding_grad, weight_grad)
```

```python
import functools

import jax
import jax.numpy as jnp
from jax import lax
from jax.experimental import pallas as pl
from jax.experimental.pallas import tpu as pltpu
from jax.sharding import PartitionSpec as P

HD = 128
SPAN = 64
NROWS = 128
NBR = 2
REACH = 2
GATHER_LIMIT = 8
VMEM_BYTES = 56 * 1024 * 1024
MESH = pl.DeviceIdType.MESH


def gather_kernel(
    n, m, w_ref, e_ref, q_ref, c_ref, p_ref, w_all, e_all, q_all, c_all, p_all,
    send_sems, recv_sems, share_send, share_recv, own_sems,
):
    me = lax.axis_index("dp")
    mp = lax.axis_index("mp")
    half = n // 2
    depth = me // 2
    side = me % 2
    ring = depth + side * (n - 1 - 2 * depth)
    part = e_ref.shape[0] // m

    def at(position):
        position = (position + 2 * n) % n
        upper = position // half
        return (1 - upper) * 2 * position + upper * (2 * (n - 1 - position) + 1)

    targets = (at(ring + 1), at(ring - 1))
    barrier = pltpu.get_barrier_semaphore()
    for target in targets:
        pl.semaphore_signal(barrier, inc=1, device_id=(target, mp), device_id_type=MESH)
    for k in range(1, m):
        pl.semaphore_signal(barrier, inc=1, device_id=(me, (mp + k) % m), device_id_type=MESH)
    pl.semaphore_wait(barrier, m + 1)

    own_rows = pl.ds(mp * part, part)
    sources = (w_ref, e_ref.at[own_rows], p_ref, q_ref, c_ref)

    def view(a, slot):
        if a == 1:
            return e_all.at[slot, own_rows]
        return (w_all, None, p_all, q_all, c_all)[a].at[slot]

    def travels(d, step, a):
        if step < half:
            return True
        return step == half and (a < 3) == (d == 0)

    def slot_of(d, step):
        return at(ring - step) if d == 0 else at(ring + step)

    def send(d, step, a):
        slot = slot_of(d, step - 1)
        return pltpu.make_async_remote_copy(
            src_ref=sources[a] if step == 1 else view(a, slot),
            dst_ref=view(a, slot),
            send_sem=send_sems.at[d, step - 1, a],
            recv_sem=recv_sems.at[d, step - 1, a],
            device_id=(targets[d], mp),
            device_id_type=MESH,
        )

    def arrival(d, step, a):
        slot = slot_of(d, step)
        return pltpu.make_async_remote_copy(
            src_ref=view(a, slot),
            dst_ref=view(a, slot),
            send_sem=send_sems.at[d, step - 1, a],
            recv_sem=recv_sems.at[d, step - 1, a],
            device_id=(targets[d], mp),
            device_id_type=MESH,
        )

    def share(d, step, k, arriving):
        slot = slot_of(d, step)
        row = (mp + m - k) % m if arriving else mp
        block = e_all.at[slot, pl.ds(row * part, part)]
        return pltpu.make_async_remote_copy(
            src_ref=block,
            dst_ref=block,
            send_sem=share_send.at[d, step - 1, k - 1],
            recv_sem=share_recv.at[d, step - 1, k - 1],
            device_id=(me, (mp + k) % m),
            device_id_type=MESH,
        )

    sent = []
    shared = []
    for a in range(5):
        for d in range(2):
            copy = send(d, 1, a)
            copy.start()
            sent.append(copy)
    own = [
        pltpu.make_async_copy(source, whole.at[me], own_sems.at[i])
        for i, (source, whole) in enumerate(
            ((w_ref, w_all), (e_ref, e_all), (p_ref, p_all), (q_ref, q_all), (c_ref, c_all))
        )
    ]
    for copy in own:
        copy.start()
    for step in range(1, half + 1):
        for a in range(5):
            for d in range(2):
                if not travels(d, step, a):
                    continue
                arrival(d, step, a).wait_recv()
                if travels(d, step + 1, a):
                    copy = send(d, step + 1, a)
                    copy.start()
                    sent.append(copy)
                if a == 1:
                    for k in range(1, m):
                        copy = share(d, step, k, False)
                        copy.start()
                        shared.append((copy, d, step, k))
    for copy, d, step, k in shared:
        share(d, step, k, True).wait_recv()
    for copy, d, step, k in shared:
        copy.wait_send()
    for copy in sent:
        copy.wait_send()
    for copy in own:
        copy.wait()


def gather(n, m, w, e, q, c, p):
    half = n // 2
    arrays = (w, e, p, q, c)
    any_spec = pl.BlockSpec(memory_space=pl.ANY)
    return pl.pallas_call(
        functools.partial(gather_kernel, n, m),
        out_shape=[jax.ShapeDtypeStruct((n,) + x.shape, x.dtype) for x in (w, e, q, c, p)],
        in_specs=[any_spec] * 5,
        out_specs=[any_spec] * 5,
        scratch_shapes=[
            pltpu.SemaphoreType.DMA((2, half, 5)),
            pltpu.SemaphoreType.DMA((2, half, 5)),
            pltpu.SemaphoreType.DMA((2, half, m - 1)),
            pltpu.SemaphoreType.DMA((2, half, m - 1)),
            pltpu.SemaphoreType.DMA((5,)),
        ],
        compiler_params=pltpu.CompilerParams(collective_id=0, has_side_effects=True),
        name="gather_inputs",
    )(w, e, q, c, p)


def dot(a, b, da, db):
    return lax.dot_general(a, b, (((da,), (db,)), ((), ())), preferred_element_type=jnp.float32)


def local_kernel(
    n, m, p_ref, w_ref, e_ref, q_ref, c_ref, att_ref, qg_ref, part_ref, wg_ref, proj, grads, grads_b
):
    me = lax.axis_index("dp")
    width = q_ref.shape[1]
    heads = width // HD
    rows_dev = e_ref.shape[0] // n
    spans_dev = q_ref.shape[0] // n // SPAN
    factor = 1.0 / HD**0.5

    @pl.loop(0, n)
    def _(block):
        proj[block] = dot(
            e_ref[pl.ds(block * rows_dev, rows_dev), :], w_ref[...], 1, 0
        ).astype(jnp.bfloat16)
        grads[block] = jnp.zeros(grads.shape[1:], jnp.float32)

    @pl.loop(0, n * spans_dev)
    def _(span):
        owner = span // spans_dev
        inner = span % spans_dev
        first = p_ref[owner, 0, inner * NBR]
        second = p_ref[owner, 0, inner * NBR + 1]
        rows = pl.ds(span * SPAN, SPAN)
        for h in range(heads):
            cols = slice(h * HD, (h + 1) * HD)
            vcols = slice(width + h * HD, width + (h + 1) * HD)
            keys = jnp.concatenate([proj[first, :, cols], proj[second, :, cols]], axis=0)
            values = jnp.concatenate([proj[first, :, vcols], proj[second, :, vcols]], axis=0)
            query = q_ref[rows, cols]
            cot = c_ref[rows, cols]
            scores = dot(query, keys, 1, 1) * factor
            top = jnp.max(scores, axis=-1, keepdims=True)
            raised = jnp.exp(scores - top)
            probs = raised / jnp.sum(raised, axis=-1, keepdims=True)
            probs_b = probs.astype(jnp.bfloat16)
            dprobs = dot(cot, values, 1, 1)
            delta = jnp.sum(probs * dprobs, axis=-1, keepdims=True)
            dscores = (probs * (dprobs - delta) * factor).astype(jnp.bfloat16)
            key_grad = dot(dscores, query, 0, 0)
            value_grad = dot(probs_b, cot, 0, 0)
            grads[first, :, cols] += key_grad[:NROWS]
            grads[second, :, cols] += key_grad[NROWS:]
            grads[first, :, vcols] += value_grad[:NROWS]
            grads[second, :, vcols] += value_grad[NROWS:]

            @pl.when(owner == me)
            def _():
                own = pl.ds(pl.multiple_of(inner * SPAN, SPAN), SPAN)
                att_ref[own, cols] = dot(probs_b, values, 1, 0).astype(jnp.bfloat16)
                qg_ref[own, cols] = dot(dscores, keys, 1, 0).astype(jnp.bfloat16)

    @pl.loop(0, n)
    def _(block):
        grads_b[pl.ds(block * rows_dev, rows_dev), :] = grads[block].astype(jnp.bfloat16)

    own_grads = grads_b[pl.ds(me * rows_dev, rows_dev), :]
    partial = dot(own_grads, w_ref[...], 1, 1).astype(jnp.bfloat16)
    piece = part_ref.shape[2]
    for k in range(m):
        part_ref[k] = partial[:, k * piece : (k + 1) * piece]
    depth, enc = wg_ref.shape[0], e_ref.shape[1]
    picked = (
        lax.broadcasted_iota(jnp.int32, (depth, enc), 0) + me * depth
        == lax.broadcasted_iota(jnp.int32, (depth, enc), 1)
    ).astype(jnp.bfloat16)
    columns = dot(picked, e_ref[...], 1, 1).astype(jnp.bfloat16)
    wg_ref[...] = dot(columns, grads_b[...], 1, 0)


def local_part(n, m, p, w, e, q, c):
    vmem = pl.BlockSpec(memory_space=pltpu.VMEM)
    depth, width = w.shape[0] // n, q.shape[1]
    rows, tokens, enc = e.shape[0] // n, q.shape[0] // n, e.shape[1]
    return pl.pallas_call(
        functools.partial(local_kernel, n, m),
        out_shape=[
            jax.ShapeDtypeStruct((tokens, width), jnp.bfloat16),
            jax.ShapeDtypeStruct((tokens, width), jnp.bfloat16),
            jax.ShapeDtypeStruct((m, rows, enc // m), jnp.bfloat16),
            jax.ShapeDtypeStruct((depth, 2 * width), jnp.float32),
        ],
        in_specs=[pl.BlockSpec(memory_space=pltpu.SMEM)] + [vmem] * 4,
        out_specs=[vmem] * 4,
        scratch_shapes=[
            pltpu.VMEM((n, rows, 2 * width), jnp.bfloat16),
            pltpu.VMEM((n, rows, 2 * width), jnp.float32),
            pltpu.VMEM((n * rows, 2 * width), jnp.bfloat16),
        ],
        compiler_params=pltpu.CompilerParams(vmem_limit_bytes=VMEM_BYTES),
        name="attention_and_gradients",
    )(p, w, e, q, c)


def group_sum_kernel(m, part_ref, out_ref, landed, send_sems, recv_sems):
    me = lax.axis_index("dp")
    mp = lax.axis_index("mp")
    barrier = pltpu.get_barrier_semaphore()
    for k in range(1, m):
        pl.semaphore_signal(barrier, inc=1, device_id=(me, (mp + k) % m), device_id_type=MESH)
    pl.semaphore_wait(barrier, m - 1)
    copies = []
    for k in range(1, m):
        target = (mp + k) % m
        copy = pltpu.make_async_remote_copy(
            src_ref=part_ref.at[target],
            dst_ref=landed.at[k - 1],
            send_sem=send_sems.at[k - 1],
            recv_sem=recv_sems.at[k - 1],
            device_id=(me, target),
            device_id_type=MESH,
        )
        copy.start()
        copies.append(copy)
    total = part_ref[mp].astype(jnp.float32)
    for k in range(1, m):
        copies[k - 1].wait_recv()
        total = total + landed[k - 1].astype(jnp.float32)
    out_ref[...] = total.astype(out_ref.dtype)
    for copy in copies:
        copy.wait_send()


def group_sum(m, part):
    vmem = pl.BlockSpec(memory_space=pltpu.VMEM)
    return pl.pallas_call(
        functools.partial(group_sum_kernel, m),
        out_shape=jax.ShapeDtypeStruct(part.shape[1:], part.dtype),
        in_specs=[vmem],
        out_specs=vmem,
        scratch_shapes=[
            pltpu.VMEM((m - 1,) + part.shape[1:], part.dtype),
            pltpu.SemaphoreType.DMA((m - 1,)),
            pltpu.SemaphoreType.DMA((m - 1,)),
        ],
        compiler_params=pltpu.CompilerParams(collective_id=1, has_side_effects=True),
        name="group_sum",
    )(part)


def per_device_gathered(n, m, queries, encodings, kv_weight, pair_list, cotangent):
    depth, _, width = kv_weight.shape
    pairs = jnp.pad(pair_list.reshape(1, -1), ((0, 7), (0, 128 - pair_list.size)))
    w, e, q, c, p = gather(
        n, m, kv_weight.reshape(depth, 2 * width), encodings, queries, cotangent, pairs
    )
    attended, query_grad, part, weight_grad = local_part(
        n,
        m,
        p,
        w.reshape(n * depth, 2 * width),
        e.reshape(-1, e.shape[2]),
        q.reshape(-1, width),
        c.reshape(-1, width),
    )
    encoding_grad = group_sum(m, part)
    return attended, query_grad, encoding_grad, weight_grad.reshape(depth, 2, width)


def shifted(value, axis, steps):
    count = lax.axis_size(axis)
    pairs = [(source, (source + steps) % count) for source in range(count)]
    return lax.ppermute(value, axis, pairs)


def project(rows, weights):
    return jnp.einsum("re,etx->rtx", rows, weights, preferred_element_type=jnp.float32).astype(
        jnp.bfloat16
    )


def fetch_window(block, reach):
    pieces = []
    for offset in range(-reach, reach + 1):
        if offset == 0:
            pieces.append(block)
        else:
            pieces.append(shifted(block, "dp", -offset))
    return pieces


def return_grads(contrib, reach):
    total = contrib[reach]
    for offset in range(-reach, reach + 1):
        if offset != 0:
            total = total + shifted(contrib[offset + reach], "dp", offset)
    return total


def per_device(queries, encodings, kv_weight, pair_list, cotangent):
    reach = REACH
    device_count = lax.axis_size("dp")
    my_index = lax.axis_index("dp")
    factor = 1.0 / HD**0.5
    weights = lax.all_gather(kv_weight, "dp", axis=0, tiled=True)
    columns = weights.shape[2]
    heads_here = columns // HD
    owned_rows = encodings.shape[0]
    slot_count = owned_rows // NROWS
    window_size = 2 * reach + 1
    own_blocks = project(encodings, weights)
    window = jnp.stack(fetch_window(own_blocks, reach), axis=0)
    pair_ids = pair_list.reshape(-1)
    owners = pair_ids // slot_count
    slot_index = pair_ids % slot_count
    offsets = (owners - my_index + reach) % device_count
    window_index = offsets * slot_count + slot_index
    span_count = pair_list.shape[0]
    chosen = jnp.take(window, window_index, axis=0).reshape(
        span_count, NBR * NROWS, 2, heads_here, HD
    )
    keys = chosen[:, :, 0]
    values = chosen[:, :, 1]
    query_rows = queries.reshape(span_count, SPAN, heads_here, HD)
    grad_rows = cotangent.reshape(span_count, SPAN, heads_here, HD)
    scores = (
        jnp.einsum("cqhd,ckhd->chqk", query_rows, keys, preferred_element_type=jnp.float32) * factor
    )
    probs = jax.nn.softmax(scores, axis=-1)
    probs_b = probs.astype(jnp.bfloat16)
    attended = jnp.einsum(
        "chqk,ckhd->cqhd", probs_b, values, preferred_element_type=jnp.float32
    ).astype(jnp.bfloat16)
    dprobs = jnp.einsum("cqhd,ckhd->chqk", grad_rows, values, preferred_element_type=jnp.float32)
    delta = jnp.sum(probs * dprobs, axis=-1, keepdims=True)
    dscores = (probs * (dprobs - delta) * factor).astype(jnp.bfloat16)
    query_grad = jnp.einsum(
        "chqk,ckhd->cqhd", dscores, keys, preferred_element_type=jnp.float32
    ).astype(jnp.bfloat16)
    key_grad = jnp.einsum(
        "chqk,cqhd->ckhd", dscores, query_rows, preferred_element_type=jnp.float32
    )
    value_grad = jnp.einsum(
        "chqk,cqhd->ckhd", probs_b, grad_rows, preferred_element_type=jnp.float32
    )
    pair_grads = jnp.stack([key_grad, value_grad], axis=2).reshape(
        span_count * NBR, NROWS * 2 * columns
    )
    one_hot = (
        window_index[:, None] == jnp.arange(window_size * slot_count, dtype=jnp.int32)[None, :]
    ).astype(jnp.float32)
    contrib = jnp.einsum("pw,pr->wr", one_hot, pair_grads, precision=lax.Precision.HIGHEST)
    contrib = contrib.reshape(window_size, owned_rows, 2, columns)
    block_grad = return_grads([contrib[index] for index in range(window_size)], reach)
    block_grad_b = block_grad.astype(jnp.bfloat16)
    partial_sum = jnp.einsum(
        "rtx,etx->re", block_grad_b, weights, preferred_element_type=jnp.float32
    )
    encoding_grad = lax.psum_scatter(
        partial_sum.astype(jnp.bfloat16), "mp", scatter_dimension=1, tiled=True
    )
    flat_grad = block_grad_b.reshape(owned_rows, 2 * columns)
    product = jnp.einsum("rc,rx->cx", encodings, flat_grad, preferred_element_type=jnp.float32)
    weight_grad = lax.psum_scatter(
        product.reshape(kv_weight.shape[0] * lax.axis_size("dp"), 2, columns),
        "dp",
        scatter_dimension=0,
        tiled=True,
    )
    return (
        attended.reshape(span_count * SPAN, columns),
        query_grad.reshape(span_count * SPAN, columns),
        encoding_grad,
        weight_grad,
    )


def solution(mesh):
    n, m = mesh.shape["dp"], mesh.shape["mp"]
    body = per_device
    if n == GATHER_LIMIT:
        body = functools.partial(per_device_gathered, n, m)
    return jax.shard_map(
        body,
        mesh=mesh,
        in_specs=(P("dp", "mp"), P("dp", None), P("dp", None, "mp"), P("dp", None), P("dp", "mp")),
        out_specs=(P("dp", "mp"), P("dp", "mp"), P("dp", "mp"), P("dp", None, "mp")),
        check_vma=False,
    )
```

```python
import functools

import jax
import jax.numpy as jnp
from jax import lax
from jax.experimental import pallas as pl
from jax.experimental.pallas import tpu as pltpu
from jax.sharding import PartitionSpec as P

HD = 128
SPAN = 64
NROWS = 128
NBR = 2
REACH = 2
GATHER_LIMIT = 8
VMEM_BYTES = 56 * 1024 * 1024
MESH = pl.DeviceIdType.MESH


def gather_kernel(
    n, m, w_ref, e_ref, q_ref, c_ref, p_ref, w_all, e_all, q_all, c_all, p_all,
    send_sems, recv_sems, share_send, share_recv, own_sems,
):
    me = lax.axis_index("dp")
    mp = lax.axis_index("mp")
    half = n // 2
    depth = me // 2
    side = me % 2
    ring = depth + side * (n - 1 - 2 * depth)
    part = e_ref.shape[0] // m

    def at(position):
        position = (position + 2 * n) % n
        upper = position // half
        return (1 - upper) * 2 * position + upper * (2 * (n - 1 - position) + 1)

    targets = (at(ring + 1), at(ring - 1))
    barrier = pltpu.get_barrier_semaphore()
    for target in targets:
        pl.semaphore_signal(barrier, inc=1, device_id=(target, mp), device_id_type=MESH)
    for k in range(1, m):
        pl.semaphore_signal(barrier, inc=1, device_id=(me, (mp + k) % m), device_id_type=MESH)
    pl.semaphore_wait(barrier, m + 1)

    own_rows = pl.ds(mp * part, part)
    sources = (w_ref, e_ref.at[own_rows], p_ref, q_ref, c_ref)

    def view(a, slot):
        if a == 1:
            return e_all.at[slot, own_rows]
        return (w_all, None, p_all, q_all, c_all)[a].at[slot]

    def travels(d, step, a):
        if step < half:
            return True
        return step == half and (a < 3) == (d == 0)

    def slot_of(d, step):
        return at(ring - step) if d == 0 else at(ring + step)

    def send(d, step, a):
        slot = slot_of(d, step - 1)
        return pltpu.make_async_remote_copy(
            src_ref=sources[a] if step == 1 else view(a, slot),
            dst_ref=view(a, slot),
            send_sem=send_sems.at[d, step - 1, a],
            recv_sem=recv_sems.at[d, step - 1, a],
            device_id=(targets[d], mp),
            device_id_type=MESH,
        )

    def arrival(d, step, a):
        slot = slot_of(d, step)
        return pltpu.make_async_remote_copy(
            src_ref=view(a, slot),
            dst_ref=view(a, slot),
            send_sem=send_sems.at[d, step - 1, a],
            recv_sem=recv_sems.at[d, step - 1, a],
            device_id=(targets[d], mp),
            device_id_type=MESH,
        )

    def share(d, step, k, arriving):
        slot = slot_of(d, step)
        row = (mp + m - k) % m if arriving else mp
        block = e_all.at[slot, pl.ds(row * part, part)]
        return pltpu.make_async_remote_copy(
            src_ref=block,
            dst_ref=block,
            send_sem=share_send.at[d, step - 1, k - 1],
            recv_sem=share_recv.at[d, step - 1, k - 1],
            device_id=(me, (mp + k) % m),
            device_id_type=MESH,
        )

    sent = []
    shared = []
    for a in range(5):
        for d in range(2):
            copy = send(d, 1, a)
            copy.start()
            sent.append(copy)
    own = [
        pltpu.make_async_copy(source, whole.at[me], own_sems.at[i])
        for i, (source, whole) in enumerate(
            ((w_ref, w_all), (e_ref, e_all), (p_ref, p_all), (q_ref, q_all), (c_ref, c_all))
        )
    ]
    for copy in own:
        copy.start()
    for step in range(1, half + 1):
        for a in range(5):
            for d in range(2):
                if not travels(d, step, a):
                    continue
                arrival(d, step, a).wait_recv()
                if travels(d, step + 1, a):
                    copy = send(d, step + 1, a)
                    copy.start()
                    sent.append(copy)
                if a == 1:
                    for k in range(1, m):
                        copy = share(d, step, k, False)
                        copy.start()
                        shared.append((copy, d, step, k))
    for copy, d, step, k in shared:
        share(d, step, k, True).wait_recv()
    for copy, d, step, k in shared:
        copy.wait_send()
    for copy in sent:
        copy.wait_send()
    for copy in own:
        copy.wait()


def gather(n, m, w, e, q, c, p):
    half = n // 2
    arrays = (w, e, p, q, c)
    any_spec = pl.BlockSpec(memory_space=pl.ANY)
    return pl.pallas_call(
        functools.partial(gather_kernel, n, m),
        out_shape=[jax.ShapeDtypeStruct((n,) + x.shape, x.dtype) for x in (w, e, q, c, p)],
        in_specs=[any_spec] * 5,
        out_specs=[any_spec] * 5,
        scratch_shapes=[
            pltpu.SemaphoreType.DMA((2, half, 5)),
            pltpu.SemaphoreType.DMA((2, half, 5)),
            pltpu.SemaphoreType.DMA((2, half, m - 1)),
            pltpu.SemaphoreType.DMA((2, half, m - 1)),
            pltpu.SemaphoreType.DMA((5,)),
        ],
        compiler_params=pltpu.CompilerParams(collective_id=0, has_side_effects=True),
        name="gather_inputs",
    )(w, e, q, c, p)


def dot(a, b, da, db):
    return lax.dot_general(a, b, (((da,), (db,)), ((), ())), preferred_element_type=jnp.float32)


def local_kernel(
    n, m, p_ref, w_ref, e_ref, q_ref, c_ref, att_ref, qg_ref, part_ref, wg_ref,
    proj, grads, grads_b, kept,
):
    me = lax.axis_index("dp")
    width = q_ref.shape[1]
    heads = width // HD
    rows_dev = e_ref.shape[0] // n
    spans_dev = q_ref.shape[0] // n // SPAN
    factor = 1.0 / HD**0.5
    zeros = jnp.zeros((SPAN, HD), jnp.bfloat16)

    @pl.loop(0, n)
    def _(block):
        rows = dot(e_ref[pl.ds(block * rows_dev, rows_dev), :], w_ref[...], 1, 0)
        rows = rows.astype(jnp.bfloat16)
        for h in range(heads):
            for t in range(2):
                proj[block, :, (2 * h + t) * HD : (2 * h + t + 1) * HD] = rows[
                    :, t * width + h * HD : t * width + (h + 1) * HD
                ]
        grads[block] = jnp.zeros(grads.shape[1:], jnp.float32)

    @pl.loop(0, n * spans_dev)
    def _(span):
        owner = span // spans_dev
        inner = span % spans_dev
        first = p_ref[owner, 0, inner * NBR]
        second = p_ref[owner, 0, inner * NBR + 1]
        rows = pl.ds(span * SPAN, SPAN)
        both = [slice(2 * h * HD, 2 * (h + 1) * HD) for h in range(heads)]
        sides, products = [], []
        for h in range(heads):
            cols = slice(h * HD, (h + 1) * HD)
            side = jnp.concatenate(
                [
                    jnp.concatenate([q_ref[rows, cols], zeros], axis=1),
                    jnp.concatenate([zeros, c_ref[rows, cols]], axis=1),
                ],
                axis=0,
            )
            keyed = jnp.concatenate([proj[first, :, both[h]], proj[second, :, both[h]]], axis=0)
            sides.append(side)
            products.append(dot(side, keyed, 1, 1))
        scores = jnp.concatenate([x[:SPAN] for x in products], axis=0) * factor
        dprobs = jnp.concatenate([x[SPAN:] for x in products], axis=0)
        top = jnp.max(scores, axis=-1, keepdims=True)
        raised = jnp.exp(scores - top)
        probs = raised * (1.0 / jnp.sum(raised, axis=-1, keepdims=True))
        delta = jnp.sum(probs * dprobs, axis=-1, keepdims=True)
        dscores = (probs * (dprobs - delta) * factor).astype(jnp.bfloat16)
        probs_b = probs.astype(jnp.bfloat16)
        totals = []
        for h in range(heads):
            part = slice(h * SPAN, (h + 1) * SPAN)
            stacked = jnp.concatenate([dscores[part], probs_b[part]], axis=0)
            kept[span, h] = stacked
            totals.append(dot(stacked, sides[h], 0, 0))
        for h in range(heads):
            grads[first, :, both[h]] += totals[h][:NROWS]
        for h in range(heads):
            grads[second, :, both[h]] += totals[h][NROWS:]

    for inner in range(spans_dev):
        first = p_ref[me, 0, inner * NBR]
        second = p_ref[me, 0, inner * NBR + 1]
        own = slice(inner * SPAN, (inner + 1) * SPAN)
        for h in range(heads):
            cols = slice(h * HD, (h + 1) * HD)
            both_h = slice(2 * h * HD, 2 * (h + 1) * HD)
            keyed = jnp.concatenate([proj[first, :, both_h], proj[second, :, both_h]], axis=0)
            product = dot(kept[me * spans_dev + inner, h], keyed, 1, 0)
            qg_ref[own, cols] = product[:SPAN, :HD].astype(jnp.bfloat16)
            att_ref[own, cols] = product[SPAN:, HD:].astype(jnp.bfloat16)

    @pl.loop(0, n)
    def _(block):
        rows = pl.ds(block * rows_dev, rows_dev)
        for h in range(heads):
            for t in range(2):
                grads_b[rows, t * width + h * HD : t * width + (h + 1) * HD] = grads[
                    block, :, (2 * h + t) * HD : (2 * h + t + 1) * HD
                ].astype(jnp.bfloat16)

    own_grads = grads_b[pl.ds(me * rows_dev, rows_dev), :]
    partial = dot(own_grads, w_ref[...], 1, 1).astype(jnp.bfloat16)
    piece = part_ref.shape[2]
    for k in range(m):
        part_ref[k] = partial[:, k * piece : (k + 1) * piece]
    depth, enc = wg_ref.shape[0], e_ref.shape[1]
    picked = (
        lax.broadcasted_iota(jnp.int32, (depth, enc), 0) + me * depth
        == lax.broadcasted_iota(jnp.int32, (depth, enc), 1)
    ).astype(jnp.bfloat16)
    columns = dot(picked, e_ref[...], 1, 1).astype(jnp.bfloat16)
    product = dot(columns, grads_b[...], 1, 0)
    for t in range(2):
        wg_ref[:, t, :] = product[:, t * width : (t + 1) * width]


def local_part(n, m, p, w, e, q, c):
    vmem = pl.BlockSpec(memory_space=pltpu.VMEM)
    depth, width = w.shape[0] // n, q.shape[1]
    rows, tokens, enc = e.shape[0] // n, q.shape[0] // n, e.shape[1]
    heads = width // HD
    return pl.pallas_call(
        functools.partial(local_kernel, n, m),
        out_shape=[
            jax.ShapeDtypeStruct((tokens, width), jnp.bfloat16),
            jax.ShapeDtypeStruct((tokens, width), jnp.bfloat16),
            jax.ShapeDtypeStruct((m, rows, enc // m), jnp.bfloat16),
            jax.ShapeDtypeStruct((depth, 2, width), jnp.float32),
        ],
        in_specs=[pl.BlockSpec(memory_space=pltpu.SMEM)] + [vmem] * 4,
        out_specs=[vmem] * 4,
        scratch_shapes=[
            pltpu.VMEM((n, rows, 2 * width), jnp.bfloat16),
            pltpu.VMEM((n, rows, 2 * width), jnp.float32),
            pltpu.VMEM((n * rows, 2 * width), jnp.bfloat16),
            pltpu.VMEM((n * tokens // SPAN, heads, 2 * SPAN, NBR * NROWS), jnp.bfloat16),
        ],
        compiler_params=pltpu.CompilerParams(vmem_limit_bytes=VMEM_BYTES),
        name="attention_and_gradients",
    )(p, w, e, q, c)


def group_sum_kernel(m, part_ref, out_ref, landed, send_sems, recv_sems):
    me = lax.axis_index("dp")
    mp = lax.axis_index("mp")
    barrier = pltpu.get_barrier_semaphore()
    for k in range(1, m):
        pl.semaphore_signal(barrier, inc=1, device_id=(me, (mp + k) % m), device_id_type=MESH)
    pl.semaphore_wait(barrier, m - 1)
    copies = []
    for k in range(1, m):
        target = (mp + k) % m
        copy = pltpu.make_async_remote_copy(
            src_ref=part_ref.at[target],
            dst_ref=landed.at[k - 1],
            send_sem=send_sems.at[k - 1],
            recv_sem=recv_sems.at[k - 1],
            device_id=(me, target),
            device_id_type=MESH,
        )
        copy.start()
        copies.append(copy)
    total = part_ref[mp].astype(jnp.float32)
    for k in range(1, m):
        copies[k - 1].wait_recv()
        total = total + landed[k - 1].astype(jnp.float32)
    out_ref[...] = total.astype(out_ref.dtype)
    for copy in copies:
        copy.wait_send()


def group_sum(m, part):
    vmem = pl.BlockSpec(memory_space=pltpu.VMEM)
    return pl.pallas_call(
        functools.partial(group_sum_kernel, m),
        out_shape=jax.ShapeDtypeStruct(part.shape[1:], part.dtype),
        in_specs=[vmem],
        out_specs=vmem,
        scratch_shapes=[
            pltpu.VMEM((m - 1,) + part.shape[1:], part.dtype),
            pltpu.SemaphoreType.DMA((m - 1,)),
            pltpu.SemaphoreType.DMA((m - 1,)),
        ],
        compiler_params=pltpu.CompilerParams(collective_id=1, has_side_effects=True),
        name="group_sum",
    )(part)


def per_device_gathered(n, m, queries, encodings, kv_weight, pair_list, cotangent):
    depth, _, width = kv_weight.shape
    pairs = jnp.pad(pair_list.reshape(1, -1), ((0, 7), (0, 128 - pair_list.size)))
    w, e, q, c, p = gather(
        n, m, kv_weight.reshape(depth, 2 * width), encodings, queries, cotangent, pairs
    )
    attended, query_grad, part, weight_grad = local_part(
        n,
        m,
        p,
        w.reshape(n * depth, 2 * width),
        e.reshape(-1, e.shape[2]),
        q.reshape(-1, width),
        c.reshape(-1, width),
    )
    encoding_grad = group_sum(m, part)
    return attended, query_grad, encoding_grad, weight_grad


def shifted(value, axis, steps):
    count = lax.axis_size(axis)
    pairs = [(source, (source + steps) % count) for source in range(count)]
    return lax.ppermute(value, axis, pairs)


def project(rows, weights):
    return jnp.einsum("re,etx->rtx", rows, weights, preferred_element_type=jnp.float32).astype(
        jnp.bfloat16
    )


def fetch_window(block, reach):
    pieces = []
    for offset in range(-reach, reach + 1):
        if offset == 0:
            pieces.append(block)
        else:
            pieces.append(shifted(block, "dp", -offset))
    return pieces


def return_grads(contrib, reach):
    total = contrib[reach]
    for offset in range(-reach, reach + 1):
        if offset != 0:
            total = total + shifted(contrib[offset + reach], "dp", offset)
    return total


def per_device(queries, encodings, kv_weight, pair_list, cotangent):
    reach = REACH
    device_count = lax.axis_size("dp")
    my_index = lax.axis_index("dp")
    factor = 1.0 / HD**0.5
    weights = lax.all_gather(kv_weight, "dp", axis=0, tiled=True)
    columns = weights.shape[2]
    heads_here = columns // HD
    owned_rows = encodings.shape[0]
    slot_count = owned_rows // NROWS
    window_size = 2 * reach + 1
    own_blocks = project(encodings, weights)
    window = jnp.stack(fetch_window(own_blocks, reach), axis=0)
    pair_ids = pair_list.reshape(-1)
    owners = pair_ids // slot_count
    slot_index = pair_ids % slot_count
    offsets = (owners - my_index + reach) % device_count
    window_index = offsets * slot_count + slot_index
    span_count = pair_list.shape[0]
    chosen = jnp.take(window, window_index, axis=0).reshape(
        span_count, NBR * NROWS, 2, heads_here, HD
    )
    keys = chosen[:, :, 0]
    values = chosen[:, :, 1]
    query_rows = queries.reshape(span_count, SPAN, heads_here, HD)
    grad_rows = cotangent.reshape(span_count, SPAN, heads_here, HD)
    scores = (
        jnp.einsum("cqhd,ckhd->chqk", query_rows, keys, preferred_element_type=jnp.float32) * factor
    )
    probs = jax.nn.softmax(scores, axis=-1)
    probs_b = probs.astype(jnp.bfloat16)
    attended = jnp.einsum(
        "chqk,ckhd->cqhd", probs_b, values, preferred_element_type=jnp.float32
    ).astype(jnp.bfloat16)
    dprobs = jnp.einsum("cqhd,ckhd->chqk", grad_rows, values, preferred_element_type=jnp.float32)
    delta = jnp.sum(probs * dprobs, axis=-1, keepdims=True)
    dscores = (probs * (dprobs - delta) * factor).astype(jnp.bfloat16)
    query_grad = jnp.einsum(
        "chqk,ckhd->cqhd", dscores, keys, preferred_element_type=jnp.float32
    ).astype(jnp.bfloat16)
    key_grad = jnp.einsum(
        "chqk,cqhd->ckhd", dscores, query_rows, preferred_element_type=jnp.float32
    )
    value_grad = jnp.einsum(
        "chqk,cqhd->ckhd", probs_b, grad_rows, preferred_element_type=jnp.float32
    )
    pair_grads = jnp.stack([key_grad, value_grad], axis=2).reshape(
        span_count * NBR, NROWS * 2 * columns
    )
    one_hot = (
        window_index[:, None] == jnp.arange(window_size * slot_count, dtype=jnp.int32)[None, :]
    ).astype(jnp.float32)
    contrib = jnp.einsum("pw,pr->wr", one_hot, pair_grads, precision=lax.Precision.HIGHEST)
    contrib = contrib.reshape(window_size, owned_rows, 2, columns)
    block_grad = return_grads([contrib[index] for index in range(window_size)], reach)
    block_grad_b = block_grad.astype(jnp.bfloat16)
    partial_sum = jnp.einsum(
        "rtx,etx->re", block_grad_b, weights, preferred_element_type=jnp.float32
    )
    encoding_grad = lax.psum_scatter(
        partial_sum.astype(jnp.bfloat16), "mp", scatter_dimension=1, tiled=True
    )
    flat_grad = block_grad_b.reshape(owned_rows, 2 * columns)
    product = jnp.einsum("rc,rx->cx", encodings, flat_grad, preferred_element_type=jnp.float32)
    weight_grad = lax.psum_scatter(
        product.reshape(kv_weight.shape[0] * lax.axis_size("dp"), 2, columns),
        "dp",
        scatter_dimension=0,
        tiled=True,
    )
    return (
        attended.reshape(span_count * SPAN, columns),
        query_grad.reshape(span_count * SPAN, columns),
        encoding_grad,
        weight_grad,
    )


def solution(mesh):
    n, m = mesh.shape["dp"], mesh.shape["mp"]
    body = per_device
    if n == GATHER_LIMIT:
        body = functools.partial(per_device_gathered, n, m)
    return jax.shard_map(
        body,
        mesh=mesh,
        in_specs=(P("dp", "mp"), P("dp", None), P("dp", None, "mp"), P("dp", None), P("dp", "mp")),
        out_specs=(P("dp", "mp"), P("dp", "mp"), P("dp", "mp"), P("dp", None, "mp")),
        check_vma=False,
    )
```

```python
import functools

import jax
import jax.numpy as jnp
from jax import lax
from jax.experimental import pallas as pl
from jax.experimental.pallas import tpu as pltpu
from jax.sharding import PartitionSpec as P

HD = 128
SPAN = 64
NROWS = 128
NBR = 2
REACH = 2
GATHER_LIMIT = 8
VMEM_BYTES = 56 * 1024 * 1024
MESH = pl.DeviceIdType.MESH


def whole_kernel(
    n, m, w_ref, e_ref, q_ref, c_ref, p_ref, att_ref, qg_ref, eg_ref, wg_ref,
    w_all, e_all, q_all, c_all, p_all, pids, order, previous, latest,
    proj, chain, grads_b, parts, landed,
    send_sems, recv_sems, share_send, share_recv, own_sems, sum_send, sum_recv,
):
    me = lax.axis_index("dp")
    mp = lax.axis_index("mp")
    half = n // 2
    depth = me // 2
    side = me % 2
    ring = depth + side * (n - 1 - 2 * depth)
    part = e_all.shape[1] // m

    def at(position):
        position = (position + 2 * n) % n
        upper = position // half
        return (1 - upper) * 2 * position + upper * (2 * (n - 1 - position) + 1)

    targets = (at(ring + 1), at(ring - 1))
    barrier = pltpu.get_barrier_semaphore()
    for target in targets:
        pl.semaphore_signal(barrier, inc=1, device_id=(target, mp), device_id_type=MESH)
    for k in range(1, m):
        pl.semaphore_signal(barrier, inc=1, device_id=(me, (mp + k) % m), device_id_type=MESH)
    pl.semaphore_wait(barrier, m + 1)

    own_rows = pl.ds(mp * part, part)
    sources = (w_ref, e_ref.at[own_rows], p_ref, q_ref, c_ref)

    def view(a, slot):
        if a == 1:
            return e_all.at[slot, own_rows]
        return (w_all, None, p_all, q_all, c_all)[a].at[slot]

    def travels(d, step, a):
        if step < half:
            return True
        return step == half and (a < 3) == (d == 0)

    def slot_of(d, step):
        return at(ring - step) if d == 0 else at(ring + step)

    def send(d, step, a):
        slot = slot_of(d, step - 1)
        return pltpu.make_async_remote_copy(
            src_ref=sources[a] if step == 1 else view(a, slot),
            dst_ref=view(a, slot),
            send_sem=send_sems.at[d, step - 1, a],
            recv_sem=recv_sems.at[d, step - 1, a],
            device_id=(targets[d], mp),
            device_id_type=MESH,
        )

    def arrival(d, step, a):
        slot = slot_of(d, step)
        return pltpu.make_async_remote_copy(
            src_ref=view(a, slot),
            dst_ref=view(a, slot),
            send_sem=send_sems.at[d, step - 1, a],
            recv_sem=recv_sems.at[d, step - 1, a],
            device_id=(targets[d], mp),
            device_id_type=MESH,
        )

    def share(d, step, k, arriving):
        slot = slot_of(d, step)
        row = (mp + m - k) % m if arriving else mp
        block = e_all.at[slot, pl.ds(row * part, part)]
        return pltpu.make_async_remote_copy(
            src_ref=block,
            dst_ref=block,
            send_sem=share_send.at[d, step - 1, k - 1],
            recv_sem=share_recv.at[d, step - 1, k - 1],
            device_id=(me, (mp + k) % m),
            device_id_type=MESH,
        )

    sent = []
    shared = []

    def start(d, step, a):
        copy = send(d, step, a)
        copy.start()
        sent.append(copy)

    def pass_on(step, arrays):
        for a in arrays:
            for d in range(2):
                if not travels(d, step, a):
                    continue
                arrival(d, step, a).wait_recv()
                if travels(d, step + 1, a):
                    start(d, step + 1, a)
                if a == 1:
                    for k in range(1, m):
                        copy = share(d, step, k, False)
                        copy.start()
                        shared.append((copy, d, step, k))

    first_arrays, later_arrays = (2, 0, 1), (3, 4)
    for a in first_arrays + later_arrays:
        for d in range(2):
            start(d, 1, a)
    own = [
        pltpu.make_async_copy(source, whole.at[me], own_sems.at[i])
        for i, (source, whole) in enumerate(
            ((w_ref, w_all), (e_ref, e_all), (p_ref, p_all), (q_ref, q_all), (c_ref, c_all))
        )
    ]
    for copy in own:
        copy.start()

    heads = q_all.shape[2] // HD
    width = heads * HD
    spans_dev = q_all.shape[1] // SPAN
    rows_dev = e_all.shape[1]
    pair_count = n * spans_dev * NBR
    factor = 1.0 / HD**0.5
    zeros = jnp.zeros((SPAN, HD), jnp.bfloat16)
    chain[pair_count] = jnp.zeros(chain.shape[1:], jnp.float32)
    for copy in own:
        copy.wait()

    for step in range(1, half):
        pass_on(step, first_arrays)
        if step == half - 2:
            pass_on(1, later_arrays)
    pass_on(half, first_arrays)
    for _, d, step, k in shared:
        share(d, step, k, True).wait_recv()

    to_scalars = pltpu.make_async_copy(p_all, pids, own_sems.at[5])
    to_scalars.start()

    @pl.loop(0, n)
    def _(block):
        rows = dot(
            e_all[block], w_all[...].reshape(n * w_all.shape[1], 2 * width), 1, 0
        ).astype(jnp.bfloat16)
        for h in range(heads):
            for t in range(2):
                proj[block, :, (2 * h + t) * HD : (2 * h + t + 1) * HD] = rows[
                    :, t * width + h * HD : t * width + (h + 1) * HD
                ]

    to_scalars.wait()

    def owner_of(unit):
        hops = (unit + 1) // 2
        return at(ring + hops * (2 * ((unit + 1) % 2) - 1))

    def link(index, last):
        unit = index // (spans_dev * NBR)
        block = pids[owner_of(unit), 0, index % (spans_dev * NBR)]
        order[index] = block
        before = jnp.int32(pair_count)
        for number in range(n):
            before = jnp.where(block == number, last[number], before)
        previous[index] = before
        return tuple(jnp.where(block == number, index, last[number]) for number in range(n))

    last = lax.fori_loop(0, pair_count, link, (jnp.int32(pair_count),) * n)
    for number in range(n):
        latest[number] = last[number]

    def attend(unit_base, units, is_own):
        @pl.loop(0, units * spans_dev)
        def _(index):
            unit = unit_base + index // spans_dev
            inner = index % spans_dev
            owner = owner_of(unit)
            pair = (unit * spans_dev + inner) * NBR
            first, second = order[pair], order[pair + 1]
            before_first, before_second = previous[pair], previous[pair + 1]
            rows = pl.ds(pl.multiple_of(inner * SPAN, SPAN), SPAN)
            both = [slice(2 * h * HD, 2 * (h + 1) * HD) for h in range(heads)]
            sides, products = [], []
            for h in range(heads):
                cols = slice(h * HD, (h + 1) * HD)
                side = jnp.concatenate(
                    [
                        jnp.concatenate([q_all[owner, rows, cols], zeros], axis=1),
                        jnp.concatenate([zeros, c_all[owner, rows, cols]], axis=1),
                    ],
                    axis=0,
                )
                keyed = jnp.concatenate(
                    [proj[first, :, both[h]], proj[second, :, both[h]]], axis=0
                )
                sides.append(side)
                products.append(dot(side, keyed, 1, 1))
            scores = jnp.concatenate([x[:SPAN] for x in products], axis=0) * factor
            dprobs = jnp.concatenate([x[SPAN:] for x in products], axis=0)
            top = jnp.max(scores, axis=-1, keepdims=True)
            raised = jnp.exp(scores - top)
            probs = raised * (1.0 / jnp.sum(raised, axis=-1, keepdims=True))
            delta = jnp.sum(probs * dprobs, axis=-1, keepdims=True)
            dscores = (probs * (dprobs - delta) * factor).astype(jnp.bfloat16)
            probs_b = probs.astype(jnp.bfloat16)
            totals = []
            for h in range(heads):
                cut = slice(h * SPAN, (h + 1) * SPAN)
                stacked = jnp.concatenate([dscores[cut], probs_b[cut]], axis=0)
                totals.append(dot(stacked, sides[h], 0, 0))
                if is_own:
                    keyed = jnp.concatenate(
                        [proj[first, :, both[h]], proj[second, :, both[h]]], axis=0
                    )
                    product = dot(stacked, keyed, 1, 0)
                    cols = slice(h * HD, (h + 1) * HD)
                    qg_ref[rows, cols] = product[:SPAN, :HD].astype(jnp.bfloat16)
                    att_ref[rows, cols] = product[SPAN:, HD:].astype(jnp.bfloat16)
            for h in range(heads):
                chain[pair, :, both[h]] = totals[h][:NROWS] + chain[before_first, :, both[h]]
            for h in range(heads):
                chain[pair + 1, :, both[h]] = totals[h][NROWS:] + chain[before_second, :, both[h]]

    attend(0, 1, True)
    for step in range(1, half):
        if step + 1 < half:
            pass_on(step + 1, later_arrays)
        attend(2 * step - 1, 2, False)
    pass_on(half, later_arrays)
    attend(n - 1, 1, False)

    def settle(block):
        at_end = latest[block]
        rows = pl.ds(block * rows_dev, rows_dev)
        for h in range(heads):
            for t in range(2):
                grads_b[rows, t * width + h * HD : t * width + (h + 1) * HD] = chain[
                    at_end, :, (2 * h + t) * HD : (2 * h + t + 1) * HD
                ].astype(jnp.bfloat16)

    settle(me)
    own_grads = grads_b[pl.ds(me * rows_dev, rows_dev), :]
    weights = w_all[...].reshape(n * w_all.shape[1], 2 * width)
    partial = dot(weights, own_grads, 1, 1).astype(jnp.bfloat16)
    piece = parts.shape[1]
    for k in range(m):
        parts[k] = partial[k * piece : (k + 1) * piece]
    copies = []
    for k in range(1, m):
        target = (mp + k) % m
        copy = pltpu.make_async_remote_copy(
            src_ref=parts.at[target],
            dst_ref=landed.at[k - 1],
            send_sem=sum_send.at[k - 1],
            recv_sem=sum_recv.at[k - 1],
            device_id=(me, target),
            device_id_type=MESH,
        )
        copy.start()
        copies.append(copy)

    @pl.loop(1, n)
    def _(offset):
        settle((me + offset) % n)

    depth, enc = wg_ref.shape[0], e_all.shape[2]
    picked = (
        lax.broadcasted_iota(jnp.int32, (depth, enc), 0) + me * depth
        == lax.broadcasted_iota(jnp.int32, (depth, enc), 1)
    ).astype(jnp.bfloat16)
    columns = dot(picked, e_all[...].reshape(n * rows_dev, enc), 1, 1).astype(jnp.bfloat16)
    product = dot(columns, grads_b[...], 1, 0)
    for t in range(2):
        wg_ref[:, t, :] = product[:, t * width : (t + 1) * width]

    total = parts[mp].astype(jnp.float32)
    for k in range(1, m):
        copies[k - 1].wait_recv()
        total = total + landed[k - 1].astype(jnp.float32)
    eg_ref[...] = total.astype(eg_ref.dtype)
    for copy in copies:
        copy.wait_send()
    for copy, d, step, k in shared:
        copy.wait_send()
    for copy in sent:
        copy.wait_send()


def dot(a, b, da, db):
    return lax.dot_general(a, b, (((da,), (db,)), ((), ())), preferred_element_type=jnp.float32)


def whole(n, m, w, e, q, c, p):
    half = n // 2
    any_spec = pl.BlockSpec(memory_space=pl.ANY)
    vmem = pl.BlockSpec(memory_space=pltpu.VMEM)
    depth, double = w.shape
    width = q.shape[1]
    rows, enc = e.shape
    pair_count = n * (q.shape[0] // SPAN) * NBR
    arrays = (w, e, q, c, p)
    return pl.pallas_call(
        functools.partial(whole_kernel, n, m),
        out_shape=[
            jax.ShapeDtypeStruct(q.shape, jnp.bfloat16),
            jax.ShapeDtypeStruct(q.shape, jnp.bfloat16),
            jax.ShapeDtypeStruct((enc // m, rows), jnp.bfloat16),
            jax.ShapeDtypeStruct((depth, 2, width), jnp.float32),
        ],
        in_specs=[any_spec] * 5,
        out_specs=[vmem] * 4,
        scratch_shapes=[pltpu.VMEM((n,) + x.shape, x.dtype) for x in arrays]
        + [
            pltpu.SMEM((n,) + p.shape, jnp.int32),
            pltpu.SMEM((pair_count,), jnp.int32),
            pltpu.SMEM((pair_count,), jnp.int32),
            pltpu.SMEM((n,), jnp.int32),
            pltpu.VMEM((n, rows, double), jnp.bfloat16),
            pltpu.VMEM((pair_count + 1, NROWS, double), jnp.float32),
            pltpu.VMEM((n * rows, double), jnp.bfloat16),
            pltpu.VMEM((m, enc // m, rows), jnp.bfloat16),
            pltpu.VMEM((m - 1, enc // m, rows), jnp.bfloat16),
            pltpu.SemaphoreType.DMA((2, half, 5)),
            pltpu.SemaphoreType.DMA((2, half, 5)),
            pltpu.SemaphoreType.DMA((2, half, m - 1)),
            pltpu.SemaphoreType.DMA((2, half, m - 1)),
            pltpu.SemaphoreType.DMA((6,)),
            pltpu.SemaphoreType.DMA((m - 1,)),
            pltpu.SemaphoreType.DMA((m - 1,)),
        ],
        compiler_params=pltpu.CompilerParams(
            collective_id=0, has_side_effects=True, vmem_limit_bytes=VMEM_BYTES
        ),
        name="whole_step",
    )(w, e, q, c, p)


def per_device_gathered(n, m, queries, encodings, kv_weight, pair_list, cotangent):
    depth, _, width = kv_weight.shape
    pairs = jnp.pad(pair_list.reshape(1, -1), ((0, 7), (0, 128 - pair_list.size)))
    attended, query_grad, encoding_grad, weight_grad = whole(
        n, m, kv_weight.reshape(depth, 2 * width), encodings, queries, cotangent, pairs
    )
    return attended, query_grad, encoding_grad.T, weight_grad

def shifted(value, axis, steps):
    count = lax.axis_size(axis)
    pairs = [(source, (source + steps) % count) for source in range(count)]
    return lax.ppermute(value, axis, pairs)


def project(rows, weights):
    return jnp.einsum("re,etx->rtx", rows, weights, preferred_element_type=jnp.float32).astype(
        jnp.bfloat16
    )


def fetch_window(block, reach):
    pieces = []
    for offset in range(-reach, reach + 1):
        if offset == 0:
            pieces.append(block)
        else:
            pieces.append(shifted(block, "dp", -offset))
    return pieces


def return_grads(contrib, reach):
    total = contrib[reach]
    for offset in range(-reach, reach + 1):
        if offset != 0:
            total = total + shifted(contrib[offset + reach], "dp", offset)
    return total


def per_device(queries, encodings, kv_weight, pair_list, cotangent):
    reach = REACH
    device_count = lax.axis_size("dp")
    my_index = lax.axis_index("dp")
    factor = 1.0 / HD**0.5
    weights = lax.all_gather(kv_weight, "dp", axis=0, tiled=True)
    columns = weights.shape[2]
    heads_here = columns // HD
    owned_rows = encodings.shape[0]
    slot_count = owned_rows // NROWS
    window_size = 2 * reach + 1
    own_blocks = project(encodings, weights)
    window = jnp.stack(fetch_window(own_blocks, reach), axis=0)
    pair_ids = pair_list.reshape(-1)
    owners = pair_ids // slot_count
    slot_index = pair_ids % slot_count
    offsets = (owners - my_index + reach) % device_count
    window_index = offsets * slot_count + slot_index
    span_count = pair_list.shape[0]
    chosen = jnp.take(window, window_index, axis=0).reshape(
        span_count, NBR * NROWS, 2, heads_here, HD
    )
    keys = chosen[:, :, 0]
    values = chosen[:, :, 1]
    query_rows = queries.reshape(span_count, SPAN, heads_here, HD)
    grad_rows = cotangent.reshape(span_count, SPAN, heads_here, HD)
    scores = (
        jnp.einsum("cqhd,ckhd->chqk", query_rows, keys, preferred_element_type=jnp.float32) * factor
    )
    probs = jax.nn.softmax(scores, axis=-1)
    probs_b = probs.astype(jnp.bfloat16)
    attended = jnp.einsum(
        "chqk,ckhd->cqhd", probs_b, values, preferred_element_type=jnp.float32
    ).astype(jnp.bfloat16)
    dprobs = jnp.einsum("cqhd,ckhd->chqk", grad_rows, values, preferred_element_type=jnp.float32)
    delta = jnp.sum(probs * dprobs, axis=-1, keepdims=True)
    dscores = (probs * (dprobs - delta) * factor).astype(jnp.bfloat16)
    query_grad = jnp.einsum(
        "chqk,ckhd->cqhd", dscores, keys, preferred_element_type=jnp.float32
    ).astype(jnp.bfloat16)
    key_grad = jnp.einsum(
        "chqk,cqhd->ckhd", dscores, query_rows, preferred_element_type=jnp.float32
    )
    value_grad = jnp.einsum(
        "chqk,cqhd->ckhd", probs_b, grad_rows, preferred_element_type=jnp.float32
    )
    pair_grads = jnp.stack([key_grad, value_grad], axis=2).reshape(
        span_count * NBR, NROWS * 2 * columns
    )
    one_hot = (
        window_index[:, None] == jnp.arange(window_size * slot_count, dtype=jnp.int32)[None, :]
    ).astype(jnp.float32)
    contrib = jnp.einsum("pw,pr->wr", one_hot, pair_grads, precision=lax.Precision.HIGHEST)
    contrib = contrib.reshape(window_size, owned_rows, 2, columns)
    block_grad = return_grads([contrib[index] for index in range(window_size)], reach)
    block_grad_b = block_grad.astype(jnp.bfloat16)
    partial_sum = jnp.einsum(
        "rtx,etx->re", block_grad_b, weights, preferred_element_type=jnp.float32
    )
    encoding_grad = lax.psum_scatter(
        partial_sum.astype(jnp.bfloat16), "mp", scatter_dimension=1, tiled=True
    )
    flat_grad = block_grad_b.reshape(owned_rows, 2 * columns)
    product = jnp.einsum("rc,rx->cx", encodings, flat_grad, preferred_element_type=jnp.float32)
    weight_grad = lax.psum_scatter(
        product.reshape(kv_weight.shape[0] * lax.axis_size("dp"), 2, columns),
        "dp",
        scatter_dimension=0,
        tiled=True,
    )
    return (
        attended.reshape(span_count * SPAN, columns),
        query_grad.reshape(span_count * SPAN, columns),
        encoding_grad,
        weight_grad,
    )


def solution(mesh):
    n, m = mesh.shape["dp"], mesh.shape["mp"]
    body = per_device
    if n == GATHER_LIMIT:
        body = functools.partial(per_device_gathered, n, m)
    return jax.shard_map(
        body,
        mesh=mesh,
        in_specs=(P("dp", "mp"), P("dp", None), P("dp", None, "mp"), P("dp", None), P("dp", "mp")),
        out_specs=(P("dp", "mp"), P("dp", "mp"), P("dp", "mp"), P("dp", None, "mp")),
        check_vma=False,
    )
```

```python
import functools

import jax
import jax.numpy as jnp
from jax import lax
from jax.experimental import pallas as pl
from jax.experimental.pallas import tpu as pltpu
from jax.sharding import PartitionSpec as P

HD = 128
SPAN = 64
NROWS = 128
NBR = 2
REACH = 2
GATHER_LIMIT = 8
VMEM_BYTES = 56 * 1024 * 1024
MESH = pl.DeviceIdType.MESH


def whole_kernel(
    n, m, w_ref, e_ref, q_ref, c_ref, p_ref, att_ref, qg_ref, eg_ref, wg_ref,
    w_all, e_all, q_all, c_all, p_all, pids, order, previous, latest,
    proj, chain, grads_b, parts, landed,
    send_sems, recv_sems, share_send, share_recv, own_sems, sum_send, sum_recv,
):
    me = lax.axis_index("dp")
    mp = lax.axis_index("mp")
    half = n // 2
    depth = me // 2
    side = me % 2
    ring = depth + side * (n - 1 - 2 * depth)
    part = e_all.shape[1] // m

    def at(position):
        position = (position + 2 * n) % n
        upper = position // half
        return (1 - upper) * 2 * position + upper * (2 * (n - 1 - position) + 1)

    targets = (at(ring + 1), at(ring - 1))
    barrier = pltpu.get_barrier_semaphore()
    for target in targets:
        pl.semaphore_signal(barrier, inc=1, device_id=(target, mp), device_id_type=MESH)
    for k in range(1, m):
        pl.semaphore_signal(barrier, inc=1, device_id=(me, (mp + k) % m), device_id_type=MESH)
    own = [
        pltpu.make_async_copy(source, whole.at[me], own_sems.at[i])
        for i, (source, whole) in enumerate(((e_ref, e_all), (q_ref, q_all), (c_ref, c_all)))
    ]
    for copy in own:
        copy.start()
    tile = lax.broadcasted_iota(jnp.int32, p_all.shape[1:], 1)
    listed = jnp.zeros(p_all.shape[1:], jnp.int32)
    for k in range(p_ref.shape[0] * NBR):
        listed = jnp.where(tile == k, p_ref[k // NBR, k % NBR], listed)
    p_all[me] = listed
    for t in range(2):
        span_cols = w_ref.shape[2]
        w_all[me, :, t * span_cols : (t + 1) * span_cols] = w_ref[:, t, :]
    pl.semaphore_wait(barrier, m + 1)

    own_rows = pl.ds(mp * part, part)
    first_arrays, later_arrays = (2, 0, 5, 1), (3, 4)
    cut = w_all.shape[1] // 32 * 16
    sources = (None, e_ref.at[own_rows], None, q_ref, c_ref, None)

    def view(a, slot):
        if a == 0:
            return w_all.at[slot, pl.ds(0, cut)]
        if a == 5:
            return w_all.at[slot, pl.ds(cut, w_all.shape[1] - cut)]
        if a == 1:
            return e_all.at[slot, own_rows]
        return (p_all, q_all, c_all)[a - 2].at[slot]

    def travels(d, step, a):
        if step < half:
            return True
        return step == half and (a not in later_arrays) == (d == 0)

    def slot_of(d, step):
        return at(ring - step) if d == 0 else at(ring + step)

    def send(d, step, a):
        slot = slot_of(d, step - 1)
        return pltpu.make_async_remote_copy(
            src_ref=view(a, slot) if step > 1 or sources[a] is None else sources[a],
            dst_ref=view(a, slot),
            send_sem=send_sems.at[d, step - 1, a],
            recv_sem=recv_sems.at[d, step - 1, a],
            device_id=(targets[d], mp),
            device_id_type=MESH,
        )

    def arrival(d, step, a):
        slot = slot_of(d, step)
        return pltpu.make_async_remote_copy(
            src_ref=view(a, slot),
            dst_ref=view(a, slot),
            send_sem=send_sems.at[d, step - 1, a],
            recv_sem=recv_sems.at[d, step - 1, a],
            device_id=(targets[d], mp),
            device_id_type=MESH,
        )

    def share(d, step, k, arriving):
        slot = slot_of(d, step)
        row = (mp + m - k) % m if arriving else mp
        block = e_all.at[slot, pl.ds(row * part, part)]
        return pltpu.make_async_remote_copy(
            src_ref=block,
            dst_ref=block,
            send_sem=share_send.at[d, step - 1, k - 1],
            recv_sem=share_recv.at[d, step - 1, k - 1],
            device_id=(me, (mp + k) % m),
            device_id_type=MESH,
        )

    sent = []
    shared = []

    def start(d, step, a):
        copy = send(d, step, a)
        copy.start()
        sent.append(copy)

    def pass_on(step, arrays, directions=(0, 1)):
        for a in arrays:
            for d in directions:
                if not travels(d, step, a):
                    continue
                arrival(d, step, a).wait_recv()
                if travels(d, step + 1, a):
                    start(d, step + 1, a)
                if a == 1:
                    for k in range(1, m):
                        copy = share(d, step, k, False)
                        copy.start()
                        shared.append((copy, d, step, k))

    for a in first_arrays:
        for d in range(2):
            start(d, 1, a)

    heads = q_all.shape[2] // HD
    width = heads * HD
    spans_dev = q_all.shape[1] // SPAN
    rows_dev = e_all.shape[1]
    pair_count = n * spans_dev * NBR
    factor = 1.0 / HD**0.5
    zeros = jnp.zeros((SPAN, HD), jnp.bfloat16)
    chain[pair_count] = jnp.zeros(chain.shape[1:], jnp.float32)
    for copy in own:
        copy.wait()

    for step in range(1, half):
        pass_on(step, first_arrays)
    for a in later_arrays:
        for d in (1, 0):
            start(d, 1, a)
    pass_on(half, first_arrays)
    for _, d, step, k in shared:
        share(d, step, k, True).wait_recv()

    to_scalars = pltpu.make_async_copy(p_all, pids, own_sems.at[3])
    to_scalars.start()

    def project(start_block, end_block):
        @pl.loop(start_block, end_block)
        def _(block):
            rows = dot(
                e_all[block], w_all[...].reshape(n * w_all.shape[1], 2 * width), 1, 0
            ).astype(jnp.bfloat16)
            for h in range(heads):
                for t in range(2):
                    proj[block, :, (2 * h + t) * HD : (2 * h + t + 1) * HD] = rows[
                        :, t * width + h * HD : t * width + (h + 1) * HD
                    ]

    project(0, half)
    pass_on(1, later_arrays, (1,))
    project(half, n)

    to_scalars.wait()

    def owner_of(unit):
        hops = (unit + 1) // 2
        return at(ring + hops * (1 - 2 * ((unit + 1) % 2)))

    def link(index, last):
        unit = index // (spans_dev * NBR)
        block = pids[owner_of(unit), 0, index % (spans_dev * NBR)]
        order[index] = block
        before = jnp.int32(pair_count)
        for number in range(n):
            before = jnp.where(block == number, last[number], before)
        previous[index] = before
        return tuple(jnp.where(block == number, index, last[number]) for number in range(n))

    last = lax.fori_loop(0, pair_count, link, (jnp.int32(pair_count),) * n)
    for number in range(n):
        latest[number] = last[number]

    def attend(unit_base, units, is_own):
        @pl.loop(0, units * spans_dev)
        def _(index):
            unit = unit_base + index // spans_dev
            inner = index % spans_dev
            owner = owner_of(unit)
            pair = (unit * spans_dev + inner) * NBR
            first, second = order[pair], order[pair + 1]
            before_first, before_second = previous[pair], previous[pair + 1]
            rows = pl.ds(pl.multiple_of(inner * SPAN, SPAN), SPAN)
            both = [slice(2 * h * HD, 2 * (h + 1) * HD) for h in range(heads)]
            sides, products = [], []
            for h in range(heads):
                cols = slice(h * HD, (h + 1) * HD)
                side = jnp.concatenate(
                    [
                        jnp.concatenate([q_all[owner, rows, cols], zeros], axis=1),
                        jnp.concatenate([zeros, c_all[owner, rows, cols]], axis=1),
                    ],
                    axis=0,
                )
                keyed = jnp.concatenate(
                    [proj[first, :, both[h]], proj[second, :, both[h]]], axis=0
                )
                sides.append(side)
                products.append(dot(side, keyed, 1, 1))
            scores = jnp.concatenate([x[:SPAN] for x in products], axis=0) * factor
            dprobs = jnp.concatenate([x[SPAN:] for x in products], axis=0)
            top = jnp.max(scores, axis=-1, keepdims=True)
            raised = jnp.exp(scores - top)
            probs = raised * (1.0 / jnp.sum(raised, axis=-1, keepdims=True))
            delta = jnp.sum(probs * dprobs, axis=-1, keepdims=True)
            dscores = (probs * (dprobs - delta) * factor).astype(jnp.bfloat16)
            probs_b = probs.astype(jnp.bfloat16)
            totals = []
            for h in range(heads):
                cut = slice(h * SPAN, (h + 1) * SPAN)
                stacked = jnp.concatenate([dscores[cut], probs_b[cut]], axis=0)
                totals.append(dot(stacked, sides[h], 0, 0))
                if is_own:
                    keyed = jnp.concatenate(
                        [proj[first, :, both[h]], proj[second, :, both[h]]], axis=0
                    )
                    product = dot(stacked, keyed, 1, 0)
                    cols = slice(h * HD, (h + 1) * HD)
                    qg_ref[rows, cols] = product[:SPAN, :HD].astype(jnp.bfloat16)
                    att_ref[rows, cols] = product[SPAN:, HD:].astype(jnp.bfloat16)
            for h in range(heads):
                chain[pair, :, both[h]] = totals[h][:NROWS] + chain[before_first, :, both[h]]
            for h in range(heads):
                chain[pair + 1, :, both[h]] = totals[h][NROWS:] + chain[before_second, :, both[h]]

    attend(0, 1, True)
    for step in range(1, half):
        pass_on(step, later_arrays, (0,))
        attend(2 * step - 1, 1, False)
        pass_on(step + 1, later_arrays, (1,))
        attend(2 * step, 1, False)
    attend(n - 1, 1, False)

    def settle(block):
        at_end = latest[block]
        rows = pl.ds(block * rows_dev, rows_dev)
        for h in range(heads):
            for t in range(2):
                grads_b[rows, t * width + h * HD : t * width + (h + 1) * HD] = chain[
                    at_end, :, (2 * h + t) * HD : (2 * h + t + 1) * HD
                ].astype(jnp.bfloat16)

    settle(me)
    own_grads = grads_b[pl.ds(me * rows_dev, rows_dev), :]
    weights = w_all[...].reshape(n * w_all.shape[1], 2 * width)
    partial = dot(weights, own_grads, 1, 1).astype(jnp.bfloat16)
    piece = parts.shape[1]
    for k in range(m):
        parts[k] = partial[k * piece : (k + 1) * piece]
    copies = []
    for k in range(1, m):
        target = (mp + k) % m
        copy = pltpu.make_async_remote_copy(
            src_ref=parts.at[target],
            dst_ref=landed.at[k - 1],
            send_sem=sum_send.at[k - 1],
            recv_sem=sum_recv.at[k - 1],
            device_id=(me, target),
            device_id_type=MESH,
        )
        copy.start()
        copies.append(copy)

    @pl.loop(1, n)
    def _(offset):
        settle((me + offset) % n)

    depth, enc = wg_ref.shape[0], e_all.shape[2]
    picked = (
        lax.broadcasted_iota(jnp.int32, (depth, enc), 0) + me * depth
        == lax.broadcasted_iota(jnp.int32, (depth, enc), 1)
    ).astype(jnp.bfloat16)
    columns = dot(picked, e_all[...].reshape(n * rows_dev, enc), 1, 1).astype(jnp.bfloat16)
    product = dot(columns, grads_b[...], 1, 0)
    for t in range(2):
        wg_ref[:, t, :] = product[:, t * width : (t + 1) * width]

    total = parts[mp].astype(jnp.float32)
    for k in range(1, m):
        copies[k - 1].wait_recv()
        total = total + landed[k - 1].astype(jnp.float32)
    eg_ref[...] = total.astype(eg_ref.dtype)
    for copy in copies:
        copy.wait_send()
    for copy, d, step, k in shared:
        copy.wait_send()
    for copy in sent:
        copy.wait_send()


def dot(a, b, da, db):
    return lax.dot_general(a, b, (((da,), (db,)), ((), ())), preferred_element_type=jnp.float32)


def whole(n, m, w, e, q, c, p):
    half = n // 2
    any_spec = pl.BlockSpec(memory_space=pl.ANY)
    vmem = pl.BlockSpec(memory_space=pltpu.VMEM)
    depth, _, width = w.shape
    double = 2 * width
    rows, enc = e.shape
    pair_count = n * (q.shape[0] // SPAN) * NBR
    listed = jax.ShapeDtypeStruct((8, 128), jnp.int32)
    arrays = (jax.ShapeDtypeStruct((depth, double), w.dtype), e, q, c, listed)
    return pl.pallas_call(
        functools.partial(whole_kernel, n, m),
        out_shape=[
            jax.ShapeDtypeStruct(q.shape, jnp.bfloat16),
            jax.ShapeDtypeStruct(q.shape, jnp.bfloat16),
            jax.ShapeDtypeStruct((enc // m, rows), jnp.bfloat16),
            jax.ShapeDtypeStruct((depth, 2, width), jnp.float32),
        ],
        in_specs=[vmem] + [any_spec] * 3 + [pl.BlockSpec(memory_space=pltpu.SMEM)],
        out_specs=[vmem] * 4,
        scratch_shapes=[pltpu.VMEM((n,) + x.shape, x.dtype) for x in arrays]
        + [
            pltpu.SMEM((n,) + listed.shape, jnp.int32),
            pltpu.SMEM((pair_count,), jnp.int32),
            pltpu.SMEM((pair_count,), jnp.int32),
            pltpu.SMEM((n,), jnp.int32),
            pltpu.VMEM((n, rows, double), jnp.bfloat16),
            pltpu.VMEM((pair_count + 1, NROWS, double), jnp.float32),
            pltpu.VMEM((n * rows, double), jnp.bfloat16),
            pltpu.VMEM((m, enc // m, rows), jnp.bfloat16),
            pltpu.VMEM((m - 1, enc // m, rows), jnp.bfloat16),
            pltpu.SemaphoreType.DMA((2, half, 6)),
            pltpu.SemaphoreType.DMA((2, half, 6)),
            pltpu.SemaphoreType.DMA((2, half, m - 1)),
            pltpu.SemaphoreType.DMA((2, half, m - 1)),
            pltpu.SemaphoreType.DMA((4,)),
            pltpu.SemaphoreType.DMA((m - 1,)),
            pltpu.SemaphoreType.DMA((m - 1,)),
        ],
        compiler_params=pltpu.CompilerParams(
            collective_id=0, has_side_effects=True, vmem_limit_bytes=VMEM_BYTES
        ),
        name="whole_step",
    )(w, e, q, c, p)


def per_device_gathered(n, m, queries, encodings, kv_weight, pair_list, cotangent):
    attended, query_grad, encoding_grad, weight_grad = whole(
        n, m, kv_weight, encodings, queries, cotangent, pair_list
    )
    return attended, query_grad, encoding_grad.T, weight_grad

def shifted(value, axis, steps):
    count = lax.axis_size(axis)
    pairs = [(source, (source + steps) % count) for source in range(count)]
    return lax.ppermute(value, axis, pairs)


def project(rows, weights):
    return jnp.einsum("re,etx->rtx", rows, weights, preferred_element_type=jnp.float32).astype(
        jnp.bfloat16
    )


def fetch_window(block, reach):
    pieces = []
    for offset in range(-reach, reach + 1):
        if offset == 0:
            pieces.append(block)
        else:
            pieces.append(shifted(block, "dp", -offset))
    return pieces


def return_grads(contrib, reach):
    total = contrib[reach]
    for offset in range(-reach, reach + 1):
        if offset != 0:
            total = total + shifted(contrib[offset + reach], "dp", offset)
    return total


def per_device(queries, encodings, kv_weight, pair_list, cotangent):
    reach = REACH
    device_count = lax.axis_size("dp")
    my_index = lax.axis_index("dp")
    factor = 1.0 / HD**0.5
    weights = lax.all_gather(kv_weight, "dp", axis=0, tiled=True)
    columns = weights.shape[2]
    heads_here = columns // HD
    owned_rows = encodings.shape[0]
    slot_count = owned_rows // NROWS
    window_size = 2 * reach + 1
    own_blocks = project(encodings, weights)
    window = jnp.stack(fetch_window(own_blocks, reach), axis=0)
    pair_ids = pair_list.reshape(-1)
    owners = pair_ids // slot_count
    slot_index = pair_ids % slot_count
    offsets = (owners - my_index + reach) % device_count
    window_index = offsets * slot_count + slot_index
    span_count = pair_list.shape[0]
    chosen = jnp.take(window, window_index, axis=0).reshape(
        span_count, NBR * NROWS, 2, heads_here, HD
    )
    keys = chosen[:, :, 0]
    values = chosen[:, :, 1]
    query_rows = queries.reshape(span_count, SPAN, heads_here, HD)
    grad_rows = cotangent.reshape(span_count, SPAN, heads_here, HD)
    scores = (
        jnp.einsum("cqhd,ckhd->chqk", query_rows, keys, preferred_element_type=jnp.float32) * factor
    )
    probs = jax.nn.softmax(scores, axis=-1)
    probs_b = probs.astype(jnp.bfloat16)
    attended = jnp.einsum(
        "chqk,ckhd->cqhd", probs_b, values, preferred_element_type=jnp.float32
    ).astype(jnp.bfloat16)
    dprobs = jnp.einsum("cqhd,ckhd->chqk", grad_rows, values, preferred_element_type=jnp.float32)
    delta = jnp.sum(probs * dprobs, axis=-1, keepdims=True)
    dscores = (probs * (dprobs - delta) * factor).astype(jnp.bfloat16)
    query_grad = jnp.einsum(
        "chqk,ckhd->cqhd", dscores, keys, preferred_element_type=jnp.float32
    ).astype(jnp.bfloat16)
    key_grad = jnp.einsum(
        "chqk,cqhd->ckhd", dscores, query_rows, preferred_element_type=jnp.float32
    )
    value_grad = jnp.einsum(
        "chqk,cqhd->ckhd", probs_b, grad_rows, preferred_element_type=jnp.float32
    )
    pair_grads = jnp.stack([key_grad, value_grad], axis=2).reshape(
        span_count * NBR, NROWS * 2 * columns
    )
    one_hot = (
        window_index[:, None] == jnp.arange(window_size * slot_count, dtype=jnp.int32)[None, :]
    ).astype(jnp.float32)
    contrib = jnp.einsum("pw,pr->wr", one_hot, pair_grads, precision=lax.Precision.HIGHEST)
    contrib = contrib.reshape(window_size, owned_rows, 2, columns)
    block_grad = return_grads([contrib[index] for index in range(window_size)], reach)
    block_grad_b = block_grad.astype(jnp.bfloat16)
    partial_sum = jnp.einsum(
        "rtx,etx->re", block_grad_b, weights, preferred_element_type=jnp.float32
    )
    encoding_grad = lax.psum_scatter(
        partial_sum.astype(jnp.bfloat16), "mp", scatter_dimension=1, tiled=True
    )
    flat_grad = block_grad_b.reshape(owned_rows, 2 * columns)
    product = jnp.einsum("rc,rx->cx", encodings, flat_grad, preferred_element_type=jnp.float32)
    weight_grad = lax.psum_scatter(
        product.reshape(kv_weight.shape[0] * lax.axis_size("dp"), 2, columns),
        "dp",
        scatter_dimension=0,
        tiled=True,
    )
    return (
        attended.reshape(span_count * SPAN, columns),
        query_grad.reshape(span_count * SPAN, columns),
        encoding_grad,
        weight_grad,
    )


def solution(mesh):
    n, m = mesh.shape["dp"], mesh.shape["mp"]
    body = per_device
    if n == GATHER_LIMIT:
        body = functools.partial(per_device_gathered, n, m)
    return jax.shard_map(
        body,
        mesh=mesh,
        in_specs=(P("dp", "mp"), P("dp", None), P("dp", None, "mp"), P("dp", None), P("dp", "mp")),
        out_specs=(P("dp", "mp"), P("dp", "mp"), P("dp", "mp"), P("dp", None, "mp")),
        check_vma=False,
    )
```

```python
import functools

import jax
import jax.numpy as jnp
from jax import lax
from jax.experimental import pallas as pl
from jax.experimental.pallas import tpu as pltpu
from jax.sharding import PartitionSpec as P

HD = 128
SPAN = 64
NROWS = 128
NBR = 2
REACH = 2
GATHER_LIMIT = 8
VMEM_BYTES = 56 * 1024 * 1024
MESH = pl.DeviceIdType.MESH


def whole_kernel(
    n, m, w_ref, e_ref, q_ref, c_ref, p_ref, att_ref, qg_ref, eg_ref, wg_ref,
    w_all, e_all, q_all, c_all, p_all, pids, order, previous, latest,
    proj, chain, grads_b, columns, parts, landed,
    send_sems, recv_sems, share_send, share_recv, own_sems, sum_send, sum_recv,
):
    me = lax.axis_index("dp")
    mp = lax.axis_index("mp")
    half = n // 2
    depth = me // 2
    side = me % 2
    ring = depth + side * (n - 1 - 2 * depth)
    part = e_all.shape[1] // m

    def at(position):
        position = (position + 2 * n) % n
        upper = position // half
        return (1 - upper) * 2 * position + upper * (2 * (n - 1 - position) + 1)

    targets = (at(ring + 1), at(ring - 1))
    barrier = pltpu.get_barrier_semaphore()
    for target in targets:
        pl.semaphore_signal(barrier, inc=1, device_id=(target, mp), device_id_type=MESH)
    for k in range(1, m):
        pl.semaphore_signal(barrier, inc=1, device_id=(me, (mp + k) % m), device_id_type=MESH)
    own = [
        pltpu.make_async_copy(source, whole.at[me], own_sems.at[i])
        for i, (source, whole) in enumerate(((e_ref, e_all), (q_ref, q_all), (c_ref, c_all)))
    ]
    for copy in own:
        copy.start()
    tile = lax.broadcasted_iota(jnp.int32, p_all.shape[1:], 1)
    listed = jnp.zeros(p_all.shape[1:], jnp.int32)
    for k in range(p_ref.shape[0] * NBR):
        listed = jnp.where(tile == k, p_ref[k // NBR, k % NBR], listed)
    p_all[me] = listed
    for t in range(2):
        span_cols = w_ref.shape[2]
        w_all[me, :, t * span_cols : (t + 1) * span_cols] = w_ref[:, t, :]
    pl.semaphore_wait(barrier, m + 1)

    own_rows = pl.ds(mp * part, part)
    first_arrays, later_arrays = (2, 0, 5, 1), (3, 4)
    cut = w_all.shape[1] // 32 * 16
    sources = (None, e_ref.at[own_rows], None, q_ref, c_ref, None)

    def view(a, slot):
        if a == 0:
            return w_all.at[slot, pl.ds(0, cut)]
        if a == 5:
            return w_all.at[slot, pl.ds(cut, w_all.shape[1] - cut)]
        if a == 1:
            return e_all.at[slot, own_rows]
        return (p_all, q_all, c_all)[a - 2].at[slot]

    def travels(d, step, a):
        if step < half:
            return True
        return step == half and (a in (2, 3, 5)) == (d == 0)

    def slot_of(d, step):
        return at(ring - step) if d == 0 else at(ring + step)

    def send(d, step, a):
        slot = slot_of(d, step - 1)
        return pltpu.make_async_remote_copy(
            src_ref=view(a, slot) if step > 1 or sources[a] is None else sources[a],
            dst_ref=view(a, slot),
            send_sem=send_sems.at[d, step - 1, a],
            recv_sem=recv_sems.at[d, step - 1, a],
            device_id=(targets[d], mp),
            device_id_type=MESH,
        )

    def arrival(d, step, a):
        slot = slot_of(d, step)
        return pltpu.make_async_remote_copy(
            src_ref=view(a, slot),
            dst_ref=view(a, slot),
            send_sem=send_sems.at[d, step - 1, a],
            recv_sem=recv_sems.at[d, step - 1, a],
            device_id=(targets[d], mp),
            device_id_type=MESH,
        )

    def share(d, step, k, arriving):
        slot = slot_of(d, step)
        row = (mp + m - k) % m if arriving else mp
        block = e_all.at[slot, pl.ds(row * part, part)]
        return pltpu.make_async_remote_copy(
            src_ref=block,
            dst_ref=block,
            send_sem=share_send.at[d, step - 1, k - 1],
            recv_sem=share_recv.at[d, step - 1, k - 1],
            device_id=(me, (mp + k) % m),
            device_id_type=MESH,
        )

    sent = []
    shared = []

    def start(d, step, a):
        copy = send(d, step, a)
        copy.start()
        sent.append(copy)

    def pass_on(step, arrays, directions=(0, 1)):
        for a in arrays:
            for d in directions:
                if not travels(d, step, a):
                    continue
                arrival(d, step, a).wait_recv()
                if travels(d, step + 1, a):
                    start(d, step + 1, a)
                if a == 1:
                    for k in range(1, m):
                        copy = share(d, step, k, False)
                        copy.start()
                        shared.append((copy, d, step, k))

    for a in first_arrays:
        for d in range(2):
            start(d, 1, a)

    heads = q_all.shape[2] // HD
    width = heads * HD
    spans_dev = q_all.shape[1] // SPAN
    rows_dev = e_all.shape[1]
    pair_count = n * spans_dev * NBR
    factor = 1.0 / HD**0.5
    zeros = jnp.zeros((SPAN, HD), jnp.bfloat16)
    chain[pair_count] = jnp.zeros(chain.shape[1:], jnp.float32)
    for copy in own:
        copy.wait()

    for step in range(1, half):
        pass_on(step, first_arrays)
    for a in later_arrays:
        for d in (1, 0):
            start(d, 1, a)
    pass_on(half, first_arrays)
    for _, d, step, k in shared:
        share(d, step, k, True).wait_recv()

    to_scalars = pltpu.make_async_copy(p_all, pids, own_sems.at[3])
    to_scalars.start()

    def project(start_block, end_block):
        @pl.loop(start_block, end_block)
        def _(block):
            rows = dot(
                e_all[block], w_all[...].reshape(n * w_all.shape[1], 2 * width), 1, 0
            ).astype(jnp.bfloat16)
            for h in range(heads):
                for t in range(2):
                    proj[block, :, (2 * h + t) * HD : (2 * h + t + 1) * HD] = rows[
                        :, t * width + h * HD : t * width + (h + 1) * HD
                    ]

    project(0, n)

    to_scalars.wait()

    def owner_of(unit):
        hops = (unit + 1) // 2
        return at(ring + hops * (1 - 2 * ((unit + 1) % 2)))

    def link(index, last):
        unit = index // (spans_dev * NBR)
        block = pids[owner_of(unit), 0, index % (spans_dev * NBR)]
        order[index] = block
        before = jnp.int32(pair_count)
        for number in range(n):
            before = jnp.where(block == number, last[number], before)
        previous[index] = before
        return tuple(jnp.where(block == number, index, last[number]) for number in range(n))

    last = lax.fori_loop(0, pair_count, link, (jnp.int32(pair_count),) * n)
    for number in range(n):
        latest[number] = last[number]

    def attend(unit_base, units, is_own):
        @pl.loop(0, units * spans_dev)
        def _(index):
            unit = unit_base + index // spans_dev
            inner = index % spans_dev
            owner = owner_of(unit)
            pair = (unit * spans_dev + inner) * NBR
            first, second = order[pair], order[pair + 1]
            before_first, before_second = previous[pair], previous[pair + 1]
            rows = pl.ds(pl.multiple_of(inner * SPAN, SPAN), SPAN)
            both = [slice(2 * h * HD, 2 * (h + 1) * HD) for h in range(heads)]
            sides, products = [], []
            for h in range(heads):
                cols = slice(h * HD, (h + 1) * HD)
                side = jnp.concatenate(
                    [
                        jnp.concatenate([q_all[owner, rows, cols], zeros], axis=1),
                        jnp.concatenate([zeros, c_all[owner, rows, cols]], axis=1),
                    ],
                    axis=0,
                )
                keyed = jnp.concatenate(
                    [proj[first, :, both[h]], proj[second, :, both[h]]], axis=0
                )
                sides.append(side)
                products.append(dot(side, keyed, 1, 1))
            scores = jnp.concatenate([x[:SPAN] for x in products], axis=0) * factor
            dprobs = jnp.concatenate([x[SPAN:] for x in products], axis=0)
            top = jnp.max(scores, axis=-1, keepdims=True)
            raised = jnp.exp(scores - top)
            probs = raised * (1.0 / jnp.sum(raised, axis=-1, keepdims=True))
            delta = jnp.sum(probs * dprobs, axis=-1, keepdims=True)
            dscores = (probs * (dprobs - delta) * factor).astype(jnp.bfloat16)
            probs_b = probs.astype(jnp.bfloat16)
            totals = []
            for h in range(heads):
                cut = slice(h * SPAN, (h + 1) * SPAN)
                stacked = jnp.concatenate([dscores[cut], probs_b[cut]], axis=0)
                totals.append(dot(stacked, sides[h], 0, 0))
                if is_own:
                    keyed = jnp.concatenate(
                        [proj[first, :, both[h]], proj[second, :, both[h]]], axis=0
                    )
                    product = dot(stacked, keyed, 1, 0)
                    cols = slice(h * HD, (h + 1) * HD)
                    qg_ref[rows, cols] = product[:SPAN, :HD].astype(jnp.bfloat16)
                    att_ref[rows, cols] = product[SPAN:, HD:].astype(jnp.bfloat16)
            for h in range(heads):
                chain[pair, :, both[h]] = totals[h][:NROWS] + chain[before_first, :, both[h]]
            for h in range(heads):
                chain[pair + 1, :, both[h]] = totals[h][NROWS:] + chain[before_second, :, both[h]]

    attend(0, 1, True)
    for step in range(1, half):
        pass_on(step, later_arrays)
        attend(2 * step - 1, 2, False)
    depth, enc = wg_ref.shape[0], e_all.shape[2]
    picked = (
        lax.broadcasted_iota(jnp.int32, (depth, enc), 0) + me * depth
        == lax.broadcasted_iota(jnp.int32, (depth, enc), 1)
    ).astype(jnp.bfloat16)
    columns[...] = dot(
        picked, e_all[...].reshape(n * rows_dev, enc), 1, 1
    ).astype(jnp.bfloat16)
    pass_on(half, later_arrays)
    attend(n - 1, 1, False)

    def settle(block):
        at_end = latest[block]
        rows = pl.ds(block * rows_dev, rows_dev)
        for h in range(heads):
            for t in range(2):
                grads_b[rows, t * width + h * HD : t * width + (h + 1) * HD] = chain[
                    at_end, :, (2 * h + t) * HD : (2 * h + t + 1) * HD
                ].astype(jnp.bfloat16)

    settle(me)
    own_grads = grads_b[pl.ds(me * rows_dev, rows_dev), :]
    weights = w_all[...].reshape(n * w_all.shape[1], 2 * width)
    partial = dot(weights, own_grads, 1, 1).astype(jnp.bfloat16)
    piece = parts.shape[1]
    for k in range(m):
        parts[k] = partial[k * piece : (k + 1) * piece]
    copies = []
    for k in range(1, m):
        target = (mp + k) % m
        copy = pltpu.make_async_remote_copy(
            src_ref=parts.at[target],
            dst_ref=landed.at[k - 1],
            send_sem=sum_send.at[k - 1],
            recv_sem=sum_recv.at[k - 1],
            device_id=(me, target),
            device_id_type=MESH,
        )
        copy.start()
        copies.append(copy)

    @pl.loop(1, n)
    def _(offset):
        settle((me + offset) % n)

    product = dot(columns[...], grads_b[...], 1, 0)
    for t in range(2):
        wg_ref[:, t, :] = product[:, t * width : (t + 1) * width]

    total = parts[mp].astype(jnp.float32)
    for k in range(1, m):
        copies[k - 1].wait_recv()
        total = total + landed[k - 1].astype(jnp.float32)
    eg_ref[...] = total.astype(eg_ref.dtype)
    for copy in copies:
        copy.wait_send()
    for copy, d, step, k in shared:
        copy.wait_send()
    for copy in sent:
        copy.wait_send()


def dot(a, b, da, db):
    return lax.dot_general(a, b, (((da,), (db,)), ((), ())), preferred_element_type=jnp.float32)


def whole(n, m, w, e, q, c, p):
    half = n // 2
    any_spec = pl.BlockSpec(memory_space=pl.ANY)
    vmem = pl.BlockSpec(memory_space=pltpu.VMEM)
    depth, _, width = w.shape
    double = 2 * width
    rows, enc = e.shape
    pair_count = n * (q.shape[0] // SPAN) * NBR
    listed = jax.ShapeDtypeStruct((8, 128), jnp.int32)
    arrays = (jax.ShapeDtypeStruct((depth, double), w.dtype), e, q, c, listed)
    return pl.pallas_call(
        functools.partial(whole_kernel, n, m),
        out_shape=[
            jax.ShapeDtypeStruct(q.shape, jnp.bfloat16),
            jax.ShapeDtypeStruct(q.shape, jnp.bfloat16),
            jax.ShapeDtypeStruct((enc // m, rows), jnp.bfloat16),
            jax.ShapeDtypeStruct((depth, 2, width), jnp.float32),
        ],
        in_specs=[vmem] + [any_spec] * 3 + [pl.BlockSpec(memory_space=pltpu.SMEM)],
        out_specs=[vmem] * 4,
        scratch_shapes=[pltpu.VMEM((n,) + x.shape, x.dtype) for x in arrays]
        + [
            pltpu.SMEM((n,) + listed.shape, jnp.int32),
            pltpu.SMEM((pair_count,), jnp.int32),
            pltpu.SMEM((pair_count,), jnp.int32),
            pltpu.SMEM((n,), jnp.int32),
            pltpu.VMEM((n, rows, double), jnp.bfloat16),
            pltpu.VMEM((pair_count + 1, NROWS, double), jnp.float32),
            pltpu.VMEM((n * rows, double), jnp.bfloat16),
            pltpu.VMEM((depth, n * rows), jnp.bfloat16),
            pltpu.VMEM((m, enc // m, rows), jnp.bfloat16),
            pltpu.VMEM((m - 1, enc // m, rows), jnp.bfloat16),
            pltpu.SemaphoreType.DMA((2, half, 6)),
            pltpu.SemaphoreType.DMA((2, half, 6)),
            pltpu.SemaphoreType.DMA((2, half, m - 1)),
            pltpu.SemaphoreType.DMA((2, half, m - 1)),
            pltpu.SemaphoreType.DMA((4,)),
            pltpu.SemaphoreType.DMA((m - 1,)),
            pltpu.SemaphoreType.DMA((m - 1,)),
        ],
        compiler_params=pltpu.CompilerParams(
            collective_id=0, has_side_effects=True, vmem_limit_bytes=VMEM_BYTES
        ),
        name="whole_step",
    )(w, e, q, c, p)


def hand_out_kernel(*refs):
    count = len(refs) // 2
    sems = refs[-1]
    copies = [
        pltpu.make_async_copy(refs[i], refs[count + i], sems.at[i]) for i in range(count)
    ]
    for copy in copies:
        copy.start()
    for copy in copies:
        copy.wait()


def hand_out(*arrays):
    any_spec = pl.BlockSpec(memory_space=pl.ANY)
    return pl.pallas_call(
        hand_out_kernel,
        out_shape=[jax.ShapeDtypeStruct(x.shape, x.dtype) for x in arrays],
        in_specs=[any_spec] * len(arrays),
        out_specs=[any_spec] * len(arrays),
        scratch_shapes=[pltpu.SemaphoreType.DMA((len(arrays),))],
        compiler_params=pltpu.CompilerParams(vmem_limit_bytes=62 * 1024 * 1024),
        name="hand_out",
    )(*arrays)


def per_device_gathered(n, m, queries, encodings, kv_weight, pair_list, cotangent):
    attended, query_grad, encoding_grad, weight_grad = whole(
        n, m, kv_weight, encodings, queries, cotangent, pair_list
    )
    attended, query_grad, encoding_grad, weight_grad = hand_out(
        attended, query_grad, encoding_grad, weight_grad
    )
    return attended, query_grad, encoding_grad.T, weight_grad

def shifted(value, axis, steps):
    count = lax.axis_size(axis)
    pairs = [(source, (source + steps) % count) for source in range(count)]
    return lax.ppermute(value, axis, pairs)


def project(rows, weights):
    return jnp.einsum("re,etx->rtx", rows, weights, preferred_element_type=jnp.float32).astype(
        jnp.bfloat16
    )


def fetch_window(block, reach):
    pieces = []
    for offset in range(-reach, reach + 1):
        if offset == 0:
            pieces.append(block)
        else:
            pieces.append(shifted(block, "dp", -offset))
    return pieces


def return_grads(contrib, reach):
    total = contrib[reach]
    for offset in range(-reach, reach + 1):
        if offset != 0:
            total = total + shifted(contrib[offset + reach], "dp", offset)
    return total


def per_device(queries, encodings, kv_weight, pair_list, cotangent):
    reach = REACH
    device_count = lax.axis_size("dp")
    my_index = lax.axis_index("dp")
    factor = 1.0 / HD**0.5
    weights = lax.all_gather(kv_weight, "dp", axis=0, tiled=True)
    columns = weights.shape[2]
    heads_here = columns // HD
    owned_rows = encodings.shape[0]
    slot_count = owned_rows // NROWS
    window_size = 2 * reach + 1
    own_blocks = project(encodings, weights)
    window = jnp.stack(fetch_window(own_blocks, reach), axis=0)
    pair_ids = pair_list.reshape(-1)
    owners = pair_ids // slot_count
    slot_index = pair_ids % slot_count
    offsets = (owners - my_index + reach) % device_count
    window_index = offsets * slot_count + slot_index
    span_count = pair_list.shape[0]
    chosen = jnp.take(window, window_index, axis=0).reshape(
        span_count, NBR * NROWS, 2, heads_here, HD
    )
    keys = chosen[:, :, 0]
    values = chosen[:, :, 1]
    query_rows = queries.reshape(span_count, SPAN, heads_here, HD)
    grad_rows = cotangent.reshape(span_count, SPAN, heads_here, HD)
    scores = (
        jnp.einsum("cqhd,ckhd->chqk", query_rows, keys, preferred_element_type=jnp.float32) * factor
    )
    probs = jax.nn.softmax(scores, axis=-1)
    probs_b = probs.astype(jnp.bfloat16)
    attended = jnp.einsum(
        "chqk,ckhd->cqhd", probs_b, values, preferred_element_type=jnp.float32
    ).astype(jnp.bfloat16)
    dprobs = jnp.einsum("cqhd,ckhd->chqk", grad_rows, values, preferred_element_type=jnp.float32)
    delta = jnp.sum(probs * dprobs, axis=-1, keepdims=True)
    dscores = (probs * (dprobs - delta) * factor).astype(jnp.bfloat16)
    query_grad = jnp.einsum(
        "chqk,ckhd->cqhd", dscores, keys, preferred_element_type=jnp.float32
    ).astype(jnp.bfloat16)
    key_grad = jnp.einsum(
        "chqk,cqhd->ckhd", dscores, query_rows, preferred_element_type=jnp.float32
    )
    value_grad = jnp.einsum(
        "chqk,cqhd->ckhd", probs_b, grad_rows, preferred_element_type=jnp.float32
    )
    pair_grads = jnp.stack([key_grad, value_grad], axis=2).reshape(
        span_count * NBR, NROWS * 2 * columns
    )
    one_hot = (
        window_index[:, None] == jnp.arange(window_size * slot_count, dtype=jnp.int32)[None, :]
    ).astype(jnp.float32)
    contrib = jnp.einsum("pw,pr->wr", one_hot, pair_grads, precision=lax.Precision.HIGHEST)
    contrib = contrib.reshape(window_size, owned_rows, 2, columns)
    block_grad = return_grads([contrib[index] for index in range(window_size)], reach)
    block_grad_b = block_grad.astype(jnp.bfloat16)
    partial_sum = jnp.einsum(
        "rtx,etx->re", block_grad_b, weights, preferred_element_type=jnp.float32
    )
    encoding_grad = lax.psum_scatter(
        partial_sum.astype(jnp.bfloat16), "mp", scatter_dimension=1, tiled=True
    )
    flat_grad = block_grad_b.reshape(owned_rows, 2 * columns)
    product = jnp.einsum("rc,rx->cx", encodings, flat_grad, preferred_element_type=jnp.float32)
    weight_grad = lax.psum_scatter(
        product.reshape(kv_weight.shape[0] * lax.axis_size("dp"), 2, columns),
        "dp",
        scatter_dimension=0,
        tiled=True,
    )
    return (
        attended.reshape(span_count * SPAN, columns),
        query_grad.reshape(span_count * SPAN, columns),
        encoding_grad,
        weight_grad,
    )


def solution(mesh):
    n, m = mesh.shape["dp"], mesh.shape["mp"]
    body = per_device
    if n == GATHER_LIMIT:
        body = functools.partial(per_device_gathered, n, m)
    return jax.shard_map(
        body,
        mesh=mesh,
        in_specs=(P("dp", "mp"), P("dp", None), P("dp", None, "mp"), P("dp", None), P("dp", "mp")),
        out_specs=(P("dp", "mp"), P("dp", "mp"), P("dp", "mp"), P("dp", None, "mp")),
        check_vma=False,
    )
```

```python
import functools

import jax
import jax.numpy as jnp
from jax import lax
from jax.experimental import pallas as pl
from jax.experimental.pallas import tpu as pltpu
from jax.sharding import PartitionSpec as P

HD = 128
SPAN = 64
NROWS = 128
NBR = 2
REACH = 2
GATHER_LIMIT = 8
VMEM_BYTES = 56 * 1024 * 1024
MESH = pl.DeviceIdType.MESH


def whole_kernel(
    n, m, w_ref, e_ref, q_ref, c_ref, p_ref, att_ref, qg_ref, eg_ref, wg_ref,
    w_all, e_all, q_all, c_all, p_all, pids, order, previous, latest,
    proj, chain, grads_b, columns, parts, landed,
    send_sems, recv_sems, share_send, share_recv, own_sems, sum_send, sum_recv,
):
    me = lax.axis_index("dp")
    mp = lax.axis_index("mp")
    half = n // 2
    depth = me // 2
    side = me % 2
    ring = depth + side * (n - 1 - 2 * depth)
    part = e_all.shape[1] // m

    def at(position):
        position = (position + 2 * n) % n
        upper = position // half
        return (1 - upper) * 2 * position + upper * (2 * (n - 1 - position) + 1)

    targets = (at(ring + 1), at(ring - 1))
    barrier = pltpu.get_barrier_semaphore()
    for target in targets:
        pl.semaphore_signal(barrier, inc=1, device_id=(target, mp), device_id_type=MESH)
    for k in range(1, m):
        pl.semaphore_signal(barrier, inc=1, device_id=(me, (mp + k) % m), device_id_type=MESH)
    own = [
        pltpu.make_async_copy(source, whole.at[me], own_sems.at[i])
        for i, (source, whole) in enumerate(((e_ref, e_all), (q_ref, q_all), (c_ref, c_all)))
    ]
    for copy in own:
        copy.start()
    tile = lax.broadcasted_iota(jnp.int32, p_all.shape[1:], 1)
    listed = jnp.zeros(p_all.shape[1:], jnp.int32)
    for k in range(p_ref.shape[0] * NBR):
        listed = jnp.where(tile == k, p_ref[k // NBR, k % NBR], listed)
    p_all[me] = listed
    for t in range(2):
        span_cols = w_ref.shape[2]
        w_all[me, :, t * span_cols : (t + 1) * span_cols] = w_ref[:, t, :]
    for copy in own:
        copy.wait()
    pl.semaphore_wait(barrier, m + 1)

    own_rows = pl.ds(mp * part, part)
    first_arrays, later_arrays = (2, 0, 5, 1), (3, 4)
    cut = w_all.shape[1] // 32 * 16

    def view(a, slot):
        if a == 0:
            return w_all.at[slot, pl.ds(0, cut)]
        if a == 5:
            return w_all.at[slot, pl.ds(cut, w_all.shape[1] - cut)]
        if a == 1:
            return e_all.at[slot, own_rows]
        return (p_all, q_all, c_all)[a - 2].at[slot]

    def travels(d, step, a):
        if step < half:
            return True
        return step == half and (a in (2, 3, 5)) == (d == 0)

    def slot_of(d, step):
        return at(ring - step) if d == 0 else at(ring + step)

    def send(d, step, a):
        slot = slot_of(d, step - 1)
        return pltpu.make_async_remote_copy(
            src_ref=view(a, slot),
            dst_ref=view(a, slot),
            send_sem=send_sems.at[d, step - 1, a],
            recv_sem=recv_sems.at[d, step - 1, a],
            device_id=(targets[d], mp),
            device_id_type=MESH,
        )

    def arrival(d, step, a):
        slot = slot_of(d, step)
        return pltpu.make_async_remote_copy(
            src_ref=view(a, slot),
            dst_ref=view(a, slot),
            send_sem=send_sems.at[d, step - 1, a],
            recv_sem=recv_sems.at[d, step - 1, a],
            device_id=(targets[d], mp),
            device_id_type=MESH,
        )

    def share(d, step, k, arriving):
        slot = slot_of(d, step)
        row = (mp + m - k) % m if arriving else mp
        block = e_all.at[slot, pl.ds(row * part, part)]
        return pltpu.make_async_remote_copy(
            src_ref=block,
            dst_ref=block,
            send_sem=share_send.at[d, step - 1, k - 1],
            recv_sem=share_recv.at[d, step - 1, k - 1],
            device_id=(me, (mp + k) % m),
            device_id_type=MESH,
        )

    sent = []
    shared = []

    def start(d, step, a):
        copy = send(d, step, a)
        copy.start()
        sent.append(copy)

    def pass_on(step, arrays, directions=(0, 1)):
        for a in arrays:
            for d in directions:
                if not travels(d, step, a):
                    continue
                arrival(d, step, a).wait_recv()
                if travels(d, step + 1, a):
                    start(d, step + 1, a)
                if a == 1:
                    for k in range(1, m):
                        copy = share(d, step, k, False)
                        copy.start()
                        shared.append((copy, d, step, k))

    for a in first_arrays:
        for d in range(2):
            start(d, 1, a)

    heads = q_all.shape[2] // HD
    width = heads * HD
    spans_dev = q_all.shape[1] // SPAN
    rows_dev = e_all.shape[1]
    pair_count = n * spans_dev * NBR
    factor = 1.0 / HD**0.5
    zeros = jnp.zeros((SPAN, HD), jnp.bfloat16)
    chain[pair_count] = jnp.zeros(chain.shape[1:], jnp.float32)

    for step in range(1, half):
        pass_on(step, first_arrays)
    for a in later_arrays:
        for d in (1, 0):
            start(d, 1, a)
    pass_on(half, first_arrays)
    for _, d, step, k in shared:
        share(d, step, k, True).wait_recv()

    to_scalars = pltpu.make_async_copy(p_all, pids, own_sems.at[3])
    to_scalars.start()

    def project(start_block, end_block):
        @pl.loop(start_block, end_block)
        def _(block):
            rows = dot(
                e_all[block], w_all[...].reshape(n * w_all.shape[1], 2 * width), 1, 0
            ).astype(jnp.bfloat16)
            for h in range(heads):
                for t in range(2):
                    proj[block, :, (2 * h + t) * HD : (2 * h + t + 1) * HD] = rows[
                        :, t * width + h * HD : t * width + (h + 1) * HD
                    ]

    project(0, n)

    to_scalars.wait()

    def owner_of(unit):
        hops = (unit + 1) // 2
        return at(ring + hops * (1 - 2 * ((unit + 1) % 2)))

    def link(index, last):
        unit = index // (spans_dev * NBR)
        block = pids[owner_of(unit), 0, index % (spans_dev * NBR)]
        order[index] = block
        before = jnp.int32(pair_count)
        for number in range(n):
            before = jnp.where(block == number, last[number], before)
        previous[index] = before
        return tuple(jnp.where(block == number, index, last[number]) for number in range(n))

    last = lax.fori_loop(0, pair_count, link, (jnp.int32(pair_count),) * n)
    for number in range(n):
        latest[number] = last[number]

    def attend(unit_base, units, is_own):
        @pl.loop(0, units * spans_dev)
        def _(index):
            unit = unit_base + index // spans_dev
            inner = index % spans_dev
            owner = owner_of(unit)
            pair = (unit * spans_dev + inner) * NBR
            first, second = order[pair], order[pair + 1]
            before_first, before_second = previous[pair], previous[pair + 1]
            rows = pl.ds(pl.multiple_of(inner * SPAN, SPAN), SPAN)
            both = [slice(2 * h * HD, 2 * (h + 1) * HD) for h in range(heads)]
            sides, products = [], []
            for h in range(heads):
                cols = slice(h * HD, (h + 1) * HD)
                side = jnp.concatenate(
                    [
                        jnp.concatenate([q_all[owner, rows, cols], zeros], axis=1),
                        jnp.concatenate([zeros, c_all[owner, rows, cols]], axis=1),
                    ],
                    axis=0,
                )
                keyed = jnp.concatenate(
                    [proj[first, :, both[h]], proj[second, :, both[h]]], axis=0
                )
                sides.append(side)
                products.append(dot(side, keyed, 1, 1))
            scores = jnp.concatenate([x[:SPAN] for x in products], axis=0) * factor
            dprobs = jnp.concatenate([x[SPAN:] for x in products], axis=0)
            top = jnp.max(scores, axis=-1, keepdims=True)
            raised = jnp.exp(scores - top)
            probs = raised * (1.0 / jnp.sum(raised, axis=-1, keepdims=True))
            delta = jnp.sum(probs * dprobs, axis=-1, keepdims=True)
            dscores = (probs * (dprobs - delta) * factor).astype(jnp.bfloat16)
            probs_b = probs.astype(jnp.bfloat16)
            totals = []
            for h in range(heads):
                cut = slice(h * SPAN, (h + 1) * SPAN)
                stacked = jnp.concatenate([dscores[cut], probs_b[cut]], axis=0)
                totals.append(dot(stacked, sides[h], 0, 0))
                if is_own:
                    keyed = jnp.concatenate(
                        [proj[first, :, both[h]], proj[second, :, both[h]]], axis=0
                    )
                    product = dot(stacked, keyed, 1, 0)
                    cols = slice(h * HD, (h + 1) * HD)
                    qg_ref[rows, cols] = product[:SPAN, :HD].astype(jnp.bfloat16)
                    att_ref[rows, cols] = product[SPAN:, HD:].astype(jnp.bfloat16)
            for h in range(heads):
                chain[pair, :, both[h]] = totals[h][:NROWS] + chain[before_first, :, both[h]]
            for h in range(heads):
                chain[pair + 1, :, both[h]] = totals[h][NROWS:] + chain[before_second, :, both[h]]

    attend(0, 1, True)
    for step in range(1, half):
        pass_on(step, later_arrays)
        attend(2 * step - 1, 2, False)
    depth, enc = wg_ref.shape[0], e_all.shape[2]
    picked = (
        lax.broadcasted_iota(jnp.int32, (depth, enc), 0) + me * depth
        == lax.broadcasted_iota(jnp.int32, (depth, enc), 1)
    ).astype(jnp.bfloat16)
    columns[...] = dot(
        picked, e_all[...].reshape(n * rows_dev, enc), 1, 1
    ).astype(jnp.bfloat16)
    pass_on(half, later_arrays)
    attend(n - 1, 1, False)

    def settle(block):
        at_end = latest[block]
        rows = pl.ds(block * rows_dev, rows_dev)
        for h in range(heads):
            for t in range(2):
                grads_b[rows, t * width + h * HD : t * width + (h + 1) * HD] = chain[
                    at_end, :, (2 * h + t) * HD : (2 * h + t + 1) * HD
                ].astype(jnp.bfloat16)

    settle(me)
    own_grads = grads_b[pl.ds(me * rows_dev, rows_dev), :]
    weights = w_all[...].reshape(n * w_all.shape[1], 2 * width)
    partial = dot(weights, own_grads, 1, 1).astype(jnp.bfloat16)
    piece = parts.shape[1]
    for k in range(m):
        parts[k] = partial[k * piece : (k + 1) * piece]
    copies = []
    for k in range(1, m):
        target = (mp + k) % m
        copy = pltpu.make_async_remote_copy(
            src_ref=parts.at[target],
            dst_ref=landed.at[k - 1],
            send_sem=sum_send.at[k - 1],
            recv_sem=sum_recv.at[k - 1],
            device_id=(me, target),
            device_id_type=MESH,
        )
        copy.start()
        copies.append(copy)

    @pl.loop(1, n)
    def _(offset):
        settle((me + offset) % n)

    product = dot(columns[...], grads_b[...], 1, 0)
    for t in range(2):
        wg_ref[:, t, :] = product[:, t * width : (t + 1) * width]

    total = parts[mp].astype(jnp.float32)
    for k in range(1, m):
        copies[k - 1].wait_recv()
        total = total + landed[k - 1].astype(jnp.float32)
    eg_ref[...] = total.astype(eg_ref.dtype)
    for copy in copies:
        copy.wait_send()
    for copy, d, step, k in shared:
        copy.wait_send()
    for copy in sent:
        copy.wait_send()


def dot(a, b, da, db):
    return lax.dot_general(a, b, (((da,), (db,)), ((), ())), preferred_element_type=jnp.float32)


def whole(n, m, w, e, q, c, p):
    half = n // 2
    any_spec = pl.BlockSpec(memory_space=pl.ANY)
    vmem = pl.BlockSpec(memory_space=pltpu.VMEM)
    depth, _, width = w.shape
    double = 2 * width
    rows, enc = e.shape
    pair_count = n * (q.shape[0] // SPAN) * NBR
    listed = jax.ShapeDtypeStruct((8, 128), jnp.int32)
    arrays = (jax.ShapeDtypeStruct((depth, double), w.dtype), e, q, c, listed)
    return pl.pallas_call(
        functools.partial(whole_kernel, n, m),
        out_shape=[
            jax.ShapeDtypeStruct(q.shape, jnp.bfloat16),
            jax.ShapeDtypeStruct(q.shape, jnp.bfloat16),
            jax.ShapeDtypeStruct((enc // m, rows), jnp.bfloat16),
            jax.ShapeDtypeStruct((depth, 2, width), jnp.float32),
        ],
        in_specs=[vmem] + [any_spec] * 3 + [pl.BlockSpec(memory_space=pltpu.SMEM)],
        out_specs=[vmem] * 4,
        scratch_shapes=[pltpu.VMEM((n,) + x.shape, x.dtype) for x in arrays]
        + [
            pltpu.SMEM((n,) + listed.shape, jnp.int32),
            pltpu.SMEM((pair_count,), jnp.int32),
            pltpu.SMEM((pair_count,), jnp.int32),
            pltpu.SMEM((n,), jnp.int32),
            pltpu.VMEM((n, rows, double), jnp.bfloat16),
            pltpu.VMEM((pair_count + 1, NROWS, double), jnp.float32),
            pltpu.VMEM((n * rows, double), jnp.bfloat16),
            pltpu.VMEM((depth, n * rows), jnp.bfloat16),
            pltpu.VMEM((m, enc // m, rows), jnp.bfloat16),
            pltpu.VMEM((m - 1, enc // m, rows), jnp.bfloat16),
            pltpu.SemaphoreType.DMA((2, half, 6)),
            pltpu.SemaphoreType.DMA((2, half, 6)),
            pltpu.SemaphoreType.DMA((2, half, m - 1)),
            pltpu.SemaphoreType.DMA((2, half, m - 1)),
            pltpu.SemaphoreType.DMA((4,)),
            pltpu.SemaphoreType.DMA((m - 1,)),
            pltpu.SemaphoreType.DMA((m - 1,)),
        ],
        compiler_params=pltpu.CompilerParams(
            collective_id=0, has_side_effects=True, vmem_limit_bytes=VMEM_BYTES
        ),
        name="whole_step",
    )(w, e, q, c, p)


def hand_out_kernel(*refs):
    count = len(refs) // 2
    for i in range(count):
        refs[count + i][...] = refs[i][...]


def hand_out(*arrays):
    vmem = pl.BlockSpec(memory_space=pltpu.VMEM)
    return pl.pallas_call(
        hand_out_kernel,
        out_shape=[jax.ShapeDtypeStruct(x.shape, x.dtype) for x in arrays],
        in_specs=[vmem] * len(arrays),
        out_specs=[vmem] * len(arrays),
        compiler_params=pltpu.CompilerParams(vmem_limit_bytes=VMEM_BYTES),
        name="hand_out",
    )(*arrays)


def per_device_gathered(n, m, queries, encodings, kv_weight, pair_list, cotangent):
    attended, query_grad, encoding_grad, weight_grad = whole(
        n, m, kv_weight, encodings, queries, cotangent, pair_list
    )
    attended, query_grad, encoding_grad, weight_grad = hand_out(
        attended, query_grad, encoding_grad, weight_grad
    )
    return attended, query_grad, encoding_grad.T, weight_grad

def shifted(value, axis, steps):
    count = lax.axis_size(axis)
    pairs = [(source, (source + steps) % count) for source in range(count)]
    return lax.ppermute(value, axis, pairs)


def project(rows, weights):
    return jnp.einsum("re,etx->rtx", rows, weights, preferred_element_type=jnp.float32).astype(
        jnp.bfloat16
    )


def fetch_window(block, reach):
    pieces = []
    for offset in range(-reach, reach + 1):
        if offset == 0:
            pieces.append(block)
        else:
            pieces.append(shifted(block, "dp", -offset))
    return pieces


def return_grads(contrib, reach):
    total = contrib[reach]
    for offset in range(-reach, reach + 1):
        if offset != 0:
            total = total + shifted(contrib[offset + reach], "dp", offset)
    return total


def per_device(queries, encodings, kv_weight, pair_list, cotangent):
    reach = REACH
    device_count = lax.axis_size("dp")
    my_index = lax.axis_index("dp")
    factor = 1.0 / HD**0.5
    weights = lax.all_gather(kv_weight, "dp", axis=0, tiled=True)
    columns = weights.shape[2]
    heads_here = columns // HD
    owned_rows = encodings.shape[0]
    slot_count = owned_rows // NROWS
    window_size = 2 * reach + 1
    own_blocks = project(encodings, weights)
    window = jnp.stack(fetch_window(own_blocks, reach), axis=0)
    pair_ids = pair_list.reshape(-1)
    owners = pair_ids // slot_count
    slot_index = pair_ids % slot_count
    offsets = (owners - my_index + reach) % device_count
    window_index = offsets * slot_count + slot_index
    span_count = pair_list.shape[0]
    chosen = jnp.take(window, window_index, axis=0).reshape(
        span_count, NBR * NROWS, 2, heads_here, HD
    )
    keys = chosen[:, :, 0]
    values = chosen[:, :, 1]
    query_rows = queries.reshape(span_count, SPAN, heads_here, HD)
    grad_rows = cotangent.reshape(span_count, SPAN, heads_here, HD)
    scores = (
        jnp.einsum("cqhd,ckhd->chqk", query_rows, keys, preferred_element_type=jnp.float32) * factor
    )
    probs = jax.nn.softmax(scores, axis=-1)
    probs_b = probs.astype(jnp.bfloat16)
    attended = jnp.einsum(
        "chqk,ckhd->cqhd", probs_b, values, preferred_element_type=jnp.float32
    ).astype(jnp.bfloat16)
    dprobs = jnp.einsum("cqhd,ckhd->chqk", grad_rows, values, preferred_element_type=jnp.float32)
    delta = jnp.sum(probs * dprobs, axis=-1, keepdims=True)
    dscores = (probs * (dprobs - delta) * factor).astype(jnp.bfloat16)
    query_grad = jnp.einsum(
        "chqk,ckhd->cqhd", dscores, keys, preferred_element_type=jnp.float32
    ).astype(jnp.bfloat16)
    key_grad = jnp.einsum(
        "chqk,cqhd->ckhd", dscores, query_rows, preferred_element_type=jnp.float32
    )
    value_grad = jnp.einsum(
        "chqk,cqhd->ckhd", probs_b, grad_rows, preferred_element_type=jnp.float32
    )
    pair_grads = jnp.stack([key_grad, value_grad], axis=2).reshape(
        span_count * NBR, NROWS * 2 * columns
    )
    one_hot = (
        window_index[:, None] == jnp.arange(window_size * slot_count, dtype=jnp.int32)[None, :]
    ).astype(jnp.float32)
    contrib = jnp.einsum("pw,pr->wr", one_hot, pair_grads, precision=lax.Precision.HIGHEST)
    contrib = contrib.reshape(window_size, owned_rows, 2, columns)
    block_grad = return_grads([contrib[index] for index in range(window_size)], reach)
    block_grad_b = block_grad.astype(jnp.bfloat16)
    partial_sum = jnp.einsum(
        "rtx,etx->re", block_grad_b, weights, preferred_element_type=jnp.float32
    )
    encoding_grad = lax.psum_scatter(
        partial_sum.astype(jnp.bfloat16), "mp", scatter_dimension=1, tiled=True
    )
    flat_grad = block_grad_b.reshape(owned_rows, 2 * columns)
    product = jnp.einsum("rc,rx->cx", encodings, flat_grad, preferred_element_type=jnp.float32)
    weight_grad = lax.psum_scatter(
        product.reshape(kv_weight.shape[0] * lax.axis_size("dp"), 2, columns),
        "dp",
        scatter_dimension=0,
        tiled=True,
    )
    return (
        attended.reshape(span_count * SPAN, columns),
        query_grad.reshape(span_count * SPAN, columns),
        encoding_grad,
        weight_grad,
    )


def solution(mesh):
    n, m = mesh.shape["dp"], mesh.shape["mp"]
    body = per_device
    if n == GATHER_LIMIT:
        body = functools.partial(per_device_gathered, n, m)
    return jax.shard_map(
        body,
        mesh=mesh,
        in_specs=(P("dp", "mp"), P("dp", None), P("dp", None, "mp"), P("dp", None), P("dp", "mp")),
        out_specs=(P("dp", "mp"), P("dp", "mp"), P("dp", "mp"), P("dp", None, "mp")),
        check_vma=False,
    )
```

```python
import functools

import jax
import jax.numpy as jnp
from jax import lax
from jax.experimental import pallas as pl
from jax.experimental.pallas import tpu as pltpu
from jax.sharding import PartitionSpec as P

HD = 128
SPAN = 64
NROWS = 128
NBR = 2
REACH = 2
GATHER_LIMIT = 8
VMEM_BYTES = 56 * 1024 * 1024
MESH = pl.DeviceIdType.MESH


def whole_kernel(
    n, m, w_ref, e_ref, q_ref, c_ref, p_ref, att_ref, qg_ref, eg_ref, wg_ref,
    w_all, e_all, q_all, c_all, p_all, pids, order, previous, latest,
    proj, chain, grads_b, columns, parts, landed,
    send_sems, recv_sems, share_send, share_recv, own_sems, sum_send, sum_recv,
):
    me = lax.axis_index("dp")
    mp = lax.axis_index("mp")
    half = n // 2
    depth = me // 2
    side = me % 2
    ring = depth + side * (n - 1 - 2 * depth)
    part = e_all.shape[1] // m

    def at(position):
        position = (position + 2 * n) % n
        upper = position // half
        return (1 - upper) * 2 * position + upper * (2 * (n - 1 - position) + 1)

    targets = (at(ring + 1), at(ring - 1))
    barrier = pltpu.get_barrier_semaphore()
    for target in targets:
        pl.semaphore_signal(barrier, inc=1, device_id=(target, mp), device_id_type=MESH)
    for k in range(1, m):
        pl.semaphore_signal(barrier, inc=1, device_id=(me, (mp + k) % m), device_id_type=MESH)
    own = [
        pltpu.make_async_copy(source, whole.at[me], own_sems.at[i])
        for i, (source, whole) in enumerate(((e_ref, e_all), (q_ref, q_all), (c_ref, c_all)))
    ]
    for copy in own:
        copy.start()
    tile = lax.broadcasted_iota(jnp.int32, p_all.shape[1:], 1)
    listed = jnp.zeros(p_all.shape[1:], jnp.int32)
    for k in range(p_ref.shape[0] * NBR):
        listed = jnp.where(tile == k, p_ref[k // NBR, k % NBR], listed)
    p_all[me] = listed
    for t in range(2):
        span_cols = w_ref.shape[2]
        w_all[me, :, t * span_cols : (t + 1) * span_cols] = w_ref[:, t, :]
    for copy in own:
        copy.wait()
    pl.semaphore_wait(barrier, m + 1)

    own_rows = pl.ds(mp * part, part)
    first_arrays, later_arrays = (2, 1, 0, 5), (3, 4)
    cut = w_all.shape[1] // 32 * 16

    def view(a, slot):
        if a == 0:
            return w_all.at[slot, pl.ds(0, cut)]
        if a == 5:
            return w_all.at[slot, pl.ds(cut, w_all.shape[1] - cut)]
        if a == 1:
            return e_all.at[slot, own_rows]
        return (p_all, q_all, c_all)[a - 2].at[slot]

    def travels(d, step, a):
        if step < half:
            return True
        return step == half and (a in (2, 3, 5)) == (d == 0)

    def slot_of(d, step):
        return at(ring - step) if d == 0 else at(ring + step)

    def send(d, step, a):
        slot = slot_of(d, step - 1)
        return pltpu.make_async_remote_copy(
            src_ref=view(a, slot),
            dst_ref=view(a, slot),
            send_sem=send_sems.at[d, step - 1, a],
            recv_sem=recv_sems.at[d, step - 1, a],
            device_id=(targets[d], mp),
            device_id_type=MESH,
        )

    def arrival(d, step, a):
        slot = slot_of(d, step)
        return pltpu.make_async_remote_copy(
            src_ref=view(a, slot),
            dst_ref=view(a, slot),
            send_sem=send_sems.at[d, step - 1, a],
            recv_sem=recv_sems.at[d, step - 1, a],
            device_id=(targets[d], mp),
            device_id_type=MESH,
        )

    def share(d, step, k, arriving):
        slot = slot_of(d, step)
        row = (mp + m - k) % m if arriving else mp
        block = e_all.at[slot, pl.ds(row * part, part)]
        return pltpu.make_async_remote_copy(
            src_ref=block,
            dst_ref=block,
            send_sem=share_send.at[d, step - 1, k - 1],
            recv_sem=share_recv.at[d, step - 1, k - 1],
            device_id=(me, (mp + k) % m),
            device_id_type=MESH,
        )

    sent = []
    shared = []

    def start(d, step, a):
        copy = send(d, step, a)
        copy.start()
        sent.append(copy)

    def pass_on(step, arrays, directions=(0, 1)):
        for a in arrays:
            for d in directions:
                if not travels(d, step, a):
                    continue
                arrival(d, step, a).wait_recv()
                if travels(d, step + 1, a):
                    start(d, step + 1, a)
                if a == 1:
                    for k in range(1, m):
                        copy = share(d, step, k, False)
                        copy.start()
                        shared.append((copy, d, step, k))

    for a in first_arrays:
        for d in range(2):
            start(d, 1, a)

    heads = q_all.shape[2] // HD
    width = heads * HD
    spans_dev = q_all.shape[1] // SPAN
    rows_dev = e_all.shape[1]
    pair_count = n * spans_dev * NBR
    factor = 1.0 / HD**0.5
    zeros = jnp.zeros((SPAN, HD), jnp.bfloat16)
    chain[pair_count] = jnp.zeros(chain.shape[1:], jnp.float32)

    for step in range(1, half):
        pass_on(step, first_arrays)
    for a in later_arrays:
        for d in (1, 0):
            start(d, 1, a)
    pass_on(half, first_arrays)
    for _, d, step, k in shared:
        share(d, step, k, True).wait_recv()

    to_scalars = pltpu.make_async_copy(p_all, pids, own_sems.at[3])
    to_scalars.start()

    def project(start_block, end_block):
        @pl.loop(start_block, end_block)
        def _(block):
            rows = dot(
                e_all[block], w_all[...].reshape(n * w_all.shape[1], 2 * width), 1, 0
            ).astype(jnp.bfloat16)
            for h in range(heads):
                for t in range(2):
                    proj[block, :, (2 * h + t) * HD : (2 * h + t + 1) * HD] = rows[
                        :, t * width + h * HD : t * width + (h + 1) * HD
                    ]

    project(0, n)

    to_scalars.wait()

    def owner_of(unit):
        hops = (unit + 1) // 2
        return at(ring + hops * (1 - 2 * ((unit + 1) % 2)))

    def link(index, last):
        unit = index // (spans_dev * NBR)
        block = pids[owner_of(unit), 0, index % (spans_dev * NBR)]
        order[index] = block
        before = jnp.int32(pair_count)
        for number in range(n):
            before = jnp.where(block == number, last[number], before)
        previous[index] = before
        return tuple(jnp.where(block == number, index, last[number]) for number in range(n))

    last = lax.fori_loop(0, pair_count, link, (jnp.int32(pair_count),) * n)
    for number in range(n):
        latest[number] = last[number]

    def attend(unit_base, units, is_own):
        @pl.loop(0, units * spans_dev)
        def _(index):
            unit = unit_base + index // spans_dev
            inner = index % spans_dev
            owner = owner_of(unit)
            pair = (unit * spans_dev + inner) * NBR
            first, second = order[pair], order[pair + 1]
            before_first, before_second = previous[pair], previous[pair + 1]
            rows = pl.ds(pl.multiple_of(inner * SPAN, SPAN), SPAN)
            both = [slice(2 * h * HD, 2 * (h + 1) * HD) for h in range(heads)]
            sides, products = [], []
            for h in range(heads):
                cols = slice(h * HD, (h + 1) * HD)
                side = jnp.concatenate(
                    [
                        jnp.concatenate([q_all[owner, rows, cols], zeros], axis=1),
                        jnp.concatenate([zeros, c_all[owner, rows, cols]], axis=1),
                    ],
                    axis=0,
                )
                keyed = jnp.concatenate(
                    [proj[first, :, both[h]], proj[second, :, both[h]]], axis=0
                )
                sides.append(side)
                products.append(dot(side, keyed, 1, 1))
            scores = jnp.concatenate([x[:SPAN] for x in products], axis=0) * factor
            dprobs = jnp.concatenate([x[SPAN:] for x in products], axis=0)
            top = jnp.max(scores, axis=-1, keepdims=True)
            raised = jnp.exp(scores - top)
            probs = raised * (1.0 / jnp.sum(raised, axis=-1, keepdims=True))
            delta = jnp.sum(probs * dprobs, axis=-1, keepdims=True)
            dscores = (probs * (dprobs - delta) * factor).astype(jnp.bfloat16)
            probs_b = probs.astype(jnp.bfloat16)
            totals = []
            for h in range(heads):
                cut = slice(h * SPAN, (h + 1) * SPAN)
                stacked = jnp.concatenate([dscores[cut], probs_b[cut]], axis=0)
                totals.append(dot(stacked, sides[h], 0, 0))
                if is_own:
                    keyed = jnp.concatenate(
                        [proj[first, :, both[h]], proj[second, :, both[h]]], axis=0
                    )
                    product = dot(stacked, keyed, 1, 0)
                    cols = slice(h * HD, (h + 1) * HD)
                    qg_ref[rows, cols] = product[:SPAN, :HD].astype(jnp.bfloat16)
                    att_ref[rows, cols] = product[SPAN:, HD:].astype(jnp.bfloat16)
            for h in range(heads):
                chain[pair, :, both[h]] = totals[h][:NROWS] + chain[before_first, :, both[h]]
            for h in range(heads):
                chain[pair + 1, :, both[h]] = totals[h][NROWS:] + chain[before_second, :, both[h]]

    attend(0, 1, True)
    for step in range(1, half):
        pass_on(step, later_arrays)
        attend(2 * step - 1, 2, False)
    depth, enc = wg_ref.shape[0], e_all.shape[2]
    picked = (
        lax.broadcasted_iota(jnp.int32, (depth, enc), 0) + me * depth
        == lax.broadcasted_iota(jnp.int32, (depth, enc), 1)
    ).astype(jnp.bfloat16)
    columns[...] = dot(
        picked, e_all[...].reshape(n * rows_dev, enc), 1, 1
    ).astype(jnp.bfloat16)
    pass_on(half, later_arrays)
    attend(n - 1, 1, False)

    def settle(block):
        at_end = latest[block]
        rows = pl.ds(block * rows_dev, rows_dev)
        for h in range(heads):
            for t in range(2):
                grads_b[rows, t * width + h * HD : t * width + (h + 1) * HD] = chain[
                    at_end, :, (2 * h + t) * HD : (2 * h + t + 1) * HD
                ].astype(jnp.bfloat16)

    settle(me)
    own_grads = grads_b[pl.ds(me * rows_dev, rows_dev), :]
    weights = w_all[...].reshape(n * w_all.shape[1], 2 * width)
    partial = dot(weights, own_grads, 1, 1).astype(jnp.bfloat16)
    piece = parts.shape[1]
    for k in range(m):
        parts[k] = partial[k * piece : (k + 1) * piece]
    copies = []
    for k in range(1, m):
        target = (mp + k) % m
        copy = pltpu.make_async_remote_copy(
            src_ref=parts.at[target],
            dst_ref=landed.at[k - 1],
            send_sem=sum_send.at[k - 1],
            recv_sem=sum_recv.at[k - 1],
            device_id=(me, target),
            device_id_type=MESH,
        )
        copy.start()
        copies.append(copy)

    @pl.loop(1, n)
    def _(offset):
        settle((me + offset) % n)

    product = dot(columns[...], grads_b[...], 1, 0)
    for t in range(2):
        wg_ref[:, t, :] = product[:, t * width : (t + 1) * width]

    total = parts[mp].astype(jnp.float32)
    for k in range(1, m):
        copies[k - 1].wait_recv()
        total = total + landed[k - 1].astype(jnp.float32)
    eg_ref[...] = total.astype(eg_ref.dtype)
    for copy in copies:
        copy.wait_send()
    for copy, d, step, k in shared:
        copy.wait_send()
    for copy in sent:
        copy.wait_send()


def dot(a, b, da, db):
    return lax.dot_general(a, b, (((da,), (db,)), ((), ())), preferred_element_type=jnp.float32)


def whole(n, m, w, e, q, c, p):
    half = n // 2
    any_spec = pl.BlockSpec(memory_space=pl.ANY)
    vmem = pl.BlockSpec(memory_space=pltpu.VMEM)
    depth, _, width = w.shape
    double = 2 * width
    rows, enc = e.shape
    pair_count = n * (q.shape[0] // SPAN) * NBR
    listed = jax.ShapeDtypeStruct((8, 128), jnp.int32)
    arrays = (jax.ShapeDtypeStruct((depth, double), w.dtype), e, q, c, listed)
    return pl.pallas_call(
        functools.partial(whole_kernel, n, m),
        out_shape=[
            jax.ShapeDtypeStruct(q.shape, jnp.bfloat16),
            jax.ShapeDtypeStruct(q.shape, jnp.bfloat16),
            jax.ShapeDtypeStruct((enc // m, rows), jnp.bfloat16),
            jax.ShapeDtypeStruct((depth, 2, width), jnp.float32),
        ],
        in_specs=[vmem] + [any_spec] * 3 + [pl.BlockSpec(memory_space=pltpu.SMEM)],
        out_specs=[vmem] * 4,
        scratch_shapes=[pltpu.VMEM((n,) + x.shape, x.dtype) for x in arrays]
        + [
            pltpu.SMEM((n,) + listed.shape, jnp.int32),
            pltpu.SMEM((pair_count,), jnp.int32),
            pltpu.SMEM((pair_count,), jnp.int32),
            pltpu.SMEM((n,), jnp.int32),
            pltpu.VMEM((n, rows, double), jnp.bfloat16),
            pltpu.VMEM((pair_count + 1, NROWS, double), jnp.float32),
            pltpu.VMEM((n * rows, double), jnp.bfloat16),
            pltpu.VMEM((depth, n * rows), jnp.bfloat16),
            pltpu.VMEM((m, enc // m, rows), jnp.bfloat16),
            pltpu.VMEM((m - 1, enc // m, rows), jnp.bfloat16),
            pltpu.SemaphoreType.DMA((2, half, 6)),
            pltpu.SemaphoreType.DMA((2, half, 6)),
            pltpu.SemaphoreType.DMA((2, half, m - 1)),
            pltpu.SemaphoreType.DMA((2, half, m - 1)),
            pltpu.SemaphoreType.DMA((4,)),
            pltpu.SemaphoreType.DMA((m - 1,)),
            pltpu.SemaphoreType.DMA((m - 1,)),
        ],
        compiler_params=pltpu.CompilerParams(
            collective_id=0, has_side_effects=True, vmem_limit_bytes=VMEM_BYTES
        ),
        name="whole_step",
    )(w, e, q, c, p)


def hand_out_kernel(*refs):
    count = len(refs) // 2
    for i in range(count):
        refs[count + i][...] = refs[i][...]


def hand_out(*arrays):
    vmem = pl.BlockSpec(memory_space=pltpu.VMEM)
    return pl.pallas_call(
        hand_out_kernel,
        out_shape=[jax.ShapeDtypeStruct(x.shape, x.dtype) for x in arrays],
        in_specs=[vmem] * len(arrays),
        out_specs=[vmem] * len(arrays),
        compiler_params=pltpu.CompilerParams(vmem_limit_bytes=VMEM_BYTES),
        name="hand_out",
    )(*arrays)


def per_device_gathered(n, m, queries, encodings, kv_weight, pair_list, cotangent):
    attended, query_grad, encoding_grad, weight_grad = whole(
        n, m, kv_weight, encodings, queries, cotangent, pair_list
    )
    attended, query_grad, encoding_grad, weight_grad = hand_out(
        attended, query_grad, encoding_grad, weight_grad
    )
    return attended, query_grad, encoding_grad.T, weight_grad

def shifted(value, axis, steps):
    count = lax.axis_size(axis)
    pairs = [(source, (source + steps) % count) for source in range(count)]
    return lax.ppermute(value, axis, pairs)


def project(rows, weights):
    return jnp.einsum("re,etx->rtx", rows, weights, preferred_element_type=jnp.float32).astype(
        jnp.bfloat16
    )


def fetch_window(block, reach):
    pieces = []
    for offset in range(-reach, reach + 1):
        if offset == 0:
            pieces.append(block)
        else:
            pieces.append(shifted(block, "dp", -offset))
    return pieces


def return_grads(contrib, reach):
    total = contrib[reach]
    for offset in range(-reach, reach + 1):
        if offset != 0:
            total = total + shifted(contrib[offset + reach], "dp", offset)
    return total


def per_device(queries, encodings, kv_weight, pair_list, cotangent):
    reach = REACH
    device_count = lax.axis_size("dp")
    my_index = lax.axis_index("dp")
    factor = 1.0 / HD**0.5
    weights = lax.all_gather(kv_weight, "dp", axis=0, tiled=True)
    columns = weights.shape[2]
    heads_here = columns // HD
    owned_rows = encodings.shape[0]
    slot_count = owned_rows // NROWS
    window_size = 2 * reach + 1
    own_blocks = project(encodings, weights)
    window = jnp.stack(fetch_window(own_blocks, reach), axis=0)
    pair_ids = pair_list.reshape(-1)
    owners = pair_ids // slot_count
    slot_index = pair_ids % slot_count
    offsets = (owners - my_index + reach) % device_count
    window_index = offsets * slot_count + slot_index
    span_count = pair_list.shape[0]
    chosen = jnp.take(window, window_index, axis=0).reshape(
        span_count, NBR * NROWS, 2, heads_here, HD
    )
    keys = chosen[:, :, 0]
    values = chosen[:, :, 1]
    query_rows = queries.reshape(span_count, SPAN, heads_here, HD)
    grad_rows = cotangent.reshape(span_count, SPAN, heads_here, HD)
    scores = (
        jnp.einsum("cqhd,ckhd->chqk", query_rows, keys, preferred_element_type=jnp.float32) * factor
    )
    probs = jax.nn.softmax(scores, axis=-1)
    probs_b = probs.astype(jnp.bfloat16)
    attended = jnp.einsum(
        "chqk,ckhd->cqhd", probs_b, values, preferred_element_type=jnp.float32
    ).astype(jnp.bfloat16)
    dprobs = jnp.einsum("cqhd,ckhd->chqk", grad_rows, values, preferred_element_type=jnp.float32)
    delta = jnp.sum(probs * dprobs, axis=-1, keepdims=True)
    dscores = (probs * (dprobs - delta) * factor).astype(jnp.bfloat16)
    query_grad = jnp.einsum(
        "chqk,ckhd->cqhd", dscores, keys, preferred_element_type=jnp.float32
    ).astype(jnp.bfloat16)
    key_grad = jnp.einsum(
        "chqk,cqhd->ckhd", dscores, query_rows, preferred_element_type=jnp.float32
    )
    value_grad = jnp.einsum(
        "chqk,cqhd->ckhd", probs_b, grad_rows, preferred_element_type=jnp.float32
    )
    pair_grads = jnp.stack([key_grad, value_grad], axis=2).reshape(
        span_count * NBR, NROWS * 2 * columns
    )
    one_hot = (
        window_index[:, None] == jnp.arange(window_size * slot_count, dtype=jnp.int32)[None, :]
    ).astype(jnp.float32)
    contrib = jnp.einsum("pw,pr->wr", one_hot, pair_grads, precision=lax.Precision.HIGHEST)
    contrib = contrib.reshape(window_size, owned_rows, 2, columns)
    block_grad = return_grads([contrib[index] for index in range(window_size)], reach)
    block_grad_b = block_grad.astype(jnp.bfloat16)
    partial_sum = jnp.einsum(
        "rtx,etx->re", block_grad_b, weights, preferred_element_type=jnp.float32
    )
    encoding_grad = lax.psum_scatter(
        partial_sum.astype(jnp.bfloat16), "mp", scatter_dimension=1, tiled=True
    )
    flat_grad = block_grad_b.reshape(owned_rows, 2 * columns)
    product = jnp.einsum("rc,rx->cx", encodings, flat_grad, preferred_element_type=jnp.float32)
    weight_grad = lax.psum_scatter(
        product.reshape(kv_weight.shape[0] * lax.axis_size("dp"), 2, columns),
        "dp",
        scatter_dimension=0,
        tiled=True,
    )
    return (
        attended.reshape(span_count * SPAN, columns),
        query_grad.reshape(span_count * SPAN, columns),
        encoding_grad,
        weight_grad,
    )


def solution(mesh):
    n, m = mesh.shape["dp"], mesh.shape["mp"]
    body = per_device
    if n == GATHER_LIMIT:
        body = functools.partial(per_device_gathered, n, m)
    return jax.shard_map(
        body,
        mesh=mesh,
        in_specs=(P("dp", "mp"), P("dp", None), P("dp", None, "mp"), P("dp", None), P("dp", "mp")),
        out_specs=(P("dp", "mp"), P("dp", "mp"), P("dp", "mp"), P("dp", None, "mp")),
        check_vma=False,
    )
```
